128 devices in a mesh: side: 4 (over z_hi, core), dev: 32 (over z_lo, x, y).
Axes of the slice: x: 4, y: 4, z: 4 (z_hi: 2, z_lo: 2; z = z_hi * 2 + z_lo), core: 2. Of those that a mesh axis runs over, the one named last changes fastest.
Arguments:
- query: bfloat16 [4, 32, 8, 4096], P('side', 'dev'), may hold values from -20 to 20, as said below
- new_key: bfloat16 [4, 32, 8, 1024], P('side', 'dev'), may hold values from -6 to 6
- new_value: bfloat16 [4, 32, 8, 1024], P('side', 'dev'), may hold values from -6 to 6
- cache_key: bfloat16 [4, 32, 8, 128, 1024], P('side', 'dev'), may hold values from -20 to 20, as said below
- cache_value: bfloat16 [4, 32, 8, 128, 1024], P('side', 'dev'), may hold values from -6 to 6
- lengths: int32 [4, 32, 8], P('side', 'dev'), may hold values from 2 to 128, as said below
- residual: bfloat16 [4, 32, 8, 4096], P('side', 'dev'), may hold values from -6 to 6
- norm_gain: float32 [4096], replicated, may hold values from 0.1 to 1.9
- router_weight: bfloat16 [4096, 4], replicated, may hold values from -0.09375 to 0.09375
- gate_weight: bfloat16 [4, 4096, 28672], P('side', None, 'dev'), may hold values from -0.09375 to 0.09375
- up_weight: bfloat16 [4, 4096, 28672], P('side', None, 'dev'), may hold values from -0.09375 to 0.09375
- down_weight: bfloat16 [4, 28672, 4096], P('side', 'dev'), may hold values from -0.0625 to 0.0625
- slot_rows: int32 [4, 32, 4, 8], P('side', 'dev'), may hold values from 0 to 7, as said below
- slot_count: int32 [4, 32, 4], P('side', 'dev'), may hold values from 0 to 8, as said below
Outputs:
- layer_out: bfloat16 [4, 32, 8, 4096], P('side', 'dev')
The draws below stay inside these ranges and needn't reach their ends.
Inputs may be any that keep to these rules, and one draw needn't show every extreme that they name: query: without structure in the shown draw. cache_key: without structure in the shown draw. `lengths`: row (0, 0, 0) has length 128. `slot_rows`: each row stands in exactly two lists of its device, at most once in each; the used slots list rows in ascending order; one expert, drawn from the seed, has every row of every device in its lists; unused slots hold arbitrary rows. `slot_count`: the counts of one device sum to 16.
All inputs are finite; a program needn't handle non-finite values.
Results may differ from the reference program's by a relative error of at most 0.012.
Values may be sent and summed in bfloat16 or wider, within the bound.
A program may use at most 128 MiB of HBM per device.

```python
import math
import jax
import jax.numpy as jnp
from jax import lax

D = 4096
HEADS = 32
KVH = 8
HD = 128
EXP = 4
FF = 7168
CTX = 128
ROW_DEV = 8
CAP = 8
PODS = 3
GROUPS = 96
ROWS = 768
N_SIDE = 4
N_DEV = 32


def draw_query(key, part):
    key = jax.random.fold_in(key, 11)
    return jnp.clip(jax.random.normal(key, (N_SIDE, N_DEV, ROW_DEV, HEADS * HD), jnp.float32), -6.0, 6.0).astype(jnp.bfloat16)


def draw_cache_key(key, part):
    key = jax.random.fold_in(key, 12)
    return jnp.clip(jax.random.normal(key, (N_SIDE, N_DEV, ROW_DEV, CTX, KVH * HD), jnp.float32), -6.0, 6.0).astype(jnp.bfloat16)


def draw_lengths(key, part):
    key = jax.random.fold_in(key, 13)
    drawn = jax.random.randint(key, (N_SIDE, N_DEV, ROW_DEV), 2, CTX + 1)
    return drawn.at[0, 0, 0].set(CTX).astype(jnp.int32)


def route_tables(key):
    group_total = N_SIDE * N_DEV
    key_star, key_other, key_filler = jax.random.split(key, 3)
    star = jax.random.randint(key_star, (), 0, EXP)
    offset = jax.random.randint(key_other, (group_total, ROW_DEV), 1, EXP)
    second = (star + offset) % EXP
    expert_ids = jnp.arange(EXP, dtype=jnp.int32)
    chosen = ((expert_ids[None, None, :] == star) | (expert_ids[None, None, :] == second[:, :, None])).astype(jnp.int32)
    counted = jnp.sum(chosen, axis=1)
    position = jnp.cumsum(chosen, axis=1) - chosen
    slot_ids = jnp.arange(CAP, dtype=jnp.int32)
    placed = chosen[:, :, :, None] * (position[:, :, :, None] == slot_ids[None, None, None, :]).astype(jnp.int32)
    row_ids = jnp.arange(ROW_DEV, dtype=jnp.int32)
    listed = jnp.sum(placed * row_ids[None, :, None, None], axis=1)
    filler = jax.random.randint(key_filler, (group_total, EXP, CAP), 0, ROW_DEV)
    filled = slot_ids[None, None, :] < counted[:, :, None]
    rows_out = jnp.where(filled, listed, filler).astype(jnp.int32).reshape(N_SIDE, N_DEV, EXP, CAP)
    return (rows_out, counted.astype(jnp.int32).reshape(N_SIDE, N_DEV, EXP))


def draw_slot_rows(key, part):
    tables = route_tables(key)
    return tables[0]


def draw_slot_count(key, part):
    tables = route_tables(key)
    return tables[1]


def block_scale(own_key, extent, cuts, least, largest):
    level, own = 1.0, jax.random.fold_in(own_key, 6)
    for dim, parts in cuts:
        steps = jnp.exp(jax.random.uniform(jax.random.fold_in(own, dim), (parts,), jnp.float32, least / len(cuts), largest / len(cuts)))
        level = level * jnp.repeat(steps, extent[dim] // parts).reshape([-1 if axis == dim else 1 for axis in range(len(extent))])
    return level


def scatter_about(rng, extent, deviation, limit, shards=(), kind=jnp.bfloat16):
    values = deviation * jax.random.normal(rng, extent, jnp.float32)
    if shards:
        values = values * block_scale(rng, extent, shards, -0.22, 0.18)
    return jnp.clip(values, -limit, limit).astype(kind)


def setup_inputs(seed: int = 0) -> dict:
    arg_keys = jax.random.split(jax.random.key(seed), 15)
    query = draw_query(jax.random.fold_in(arg_keys[14], 71), 0)
    new_key = scatter_about(arg_keys[1], (N_SIDE, N_DEV, ROW_DEV, KVH * HD), 1.0, 6.0, ((0, 4), (1, 32)))
    new_value = scatter_about(arg_keys[2], (N_SIDE, N_DEV, ROW_DEV, KVH * HD), 1.0, 6.0, ((0, 4), (1, 32)))
    cache_key = draw_cache_key(jax.random.fold_in(arg_keys[14], 71), 0)
    cache_value = scatter_about(arg_keys[4], (N_SIDE, N_DEV, ROW_DEV, CTX, KVH * HD), 1.0, 6.0, ((0, 4), (1, 32)))
    lengths = draw_lengths(jax.random.fold_in(arg_keys[14], 71), 0)
    residual = scatter_about(arg_keys[6], (N_SIDE, N_DEV, ROW_DEV, D), 1.0, 6.0, ((0, 4), (1, 32)))
    norm_gain = jnp.clip(1.0 + 0.18 * jax.random.normal(arg_keys[7], (D,), jnp.float32), 0.1, 1.9)
    router_weight = scatter_about(arg_keys[8], (D, EXP), D ** -0.5, 0.09375)
    gate_weight = scatter_about(arg_keys[9], (N_SIDE, D, EXP * FF), D ** -0.5, 0.09375, ((0, 4), (2, 32)))
    up_weight = scatter_about(arg_keys[10], (N_SIDE, D, EXP * FF), D ** -0.5, 0.09375, ((0, 4), (2, 32)))
    down_weight = scatter_about(arg_keys[11], (N_SIDE, EXP * FF, D), FF ** -0.5, 0.0625, ((0, 4), (1, 32)))
    slot_rows = draw_slot_rows(jax.random.fold_in(arg_keys[14], 71), 0)
    slot_count = draw_slot_count(jax.random.fold_in(arg_keys[14], 71), 0)
    return dict(query=query, new_key=new_key, new_value=new_value, cache_key=cache_key, cache_value=cache_value, lengths=lengths, residual=residual, norm_gain=norm_gain, router_weight=router_weight, gate_weight=gate_weight, up_weight=up_weight, down_weight=down_weight, slot_rows=slot_rows, slot_count=slot_count)


def attend(query, new_key, new_value, cache_key, cache_value, lengths):
    row_count = query.shape[0]
    group_size = HEADS // KVH
    queries = query.astype(jnp.float32).reshape(row_count, KVH, group_size, HD)
    keys_all = cache_key.astype(jnp.float32).reshape(row_count, CTX, KVH, HD)
    values_all = cache_value.astype(jnp.float32).reshape(row_count, CTX, KVH, HD)
    score_scale = 1.0 / math.sqrt(HD)
    scores = jnp.einsum('rkgd,rckd->rkgc', queries, keys_all) * score_scale
    own_score = jnp.einsum('rkgd,rkd->rkg', queries, new_key.astype(jnp.float32).reshape(row_count, KVH, HD)) * score_scale
    visible = jnp.arange(CTX, dtype=jnp.int32)[None, :] < lengths[:, None]
    scores = jnp.where(visible[:, None, None, :], scores, -jnp.inf)
    row_top = jnp.maximum(lax.optimization_barrier(jnp.max(scores, axis=3)), own_score)
    probs = jnp.exp(scores - row_top[..., None])
    own_prob = jnp.exp(own_score - row_top)
    denominator = lax.optimization_barrier(jnp.sum(probs, axis=3)) + own_prob
    weights = (probs / denominator[..., None]).astype(jnp.bfloat16)
    own_weight = (own_prob / denominator).astype(jnp.bfloat16)
    context = jnp.einsum('rkgc,rckd->rkgd', weights.astype(jnp.float32), values_all)
    context = context + own_weight.astype(jnp.float32)[..., None] * new_value.astype(jnp.float32).reshape(row_count, KVH, 1, HD)
    return context.reshape(row_count, HEADS * HD)

def reference(query, new_key, new_value, cache_key, cache_value, lengths, residual, norm_gain, router_weight, gate_weight, up_weight, down_weight, slot_rows, slot_count):
    q_rows = query[:PODS].reshape(ROWS, HEADS * HD)
    k_rows = new_key[:PODS].reshape(ROWS, KVH * HD)
    v_rows = new_value[:PODS].reshape(ROWS, KVH * HD)
    ck_rows = cache_key[:PODS].reshape(ROWS, CTX, KVH * HD)
    cv_rows = cache_value[:PODS].reshape(ROWS, CTX, KVH * HD)
    len_rows = lengths[:PODS].reshape(ROWS)
    res_rows = residual[:PODS].reshape(ROWS, D)
    listed = slot_rows[:PODS].reshape(GROUPS, EXP, CAP)
    counted = slot_count[:PODS].reshape(GROUPS, EXP)
    gate_all = gate_weight[PODS]
    up_all = up_weight[PODS]
    down_all = down_weight[PODS]
    context = attend(q_rows, k_rows, v_rows, ck_rows, cv_rows, len_rows)
    stream = res_rows.astype(jnp.float32) + context
    normed = (stream * lax.rsqrt(lax.optimization_barrier(jnp.mean(stream * stream, axis=1, keepdims=True)) + 1e-05) * norm_gain).astype(jnp.bfloat16)
    logits = jnp.dot(normed, router_weight, preferred_element_type=jnp.float32)
    row_ids = jnp.arange(ROW_DEV, dtype=jnp.int32)
    slot_ids = jnp.arange(CAP, dtype=jnp.int32)
    select = ((listed[:, :, :, None] == row_ids[None, None, None, :]) & (slot_ids[None, None, :, None] < counted[:, :, None, None])).astype(jnp.float32)
    chosen = jnp.transpose(lax.optimization_barrier(jnp.sum(select, axis=2)), (0, 2, 1)).reshape(ROWS, EXP)
    raised = chosen * jnp.exp(logits)
    route_weight = raised / lax.optimization_barrier(jnp.sum(raised, axis=1, keepdims=True))
    grouped = normed.astype(jnp.float32).reshape(GROUPS, ROW_DEV, D)
    slot_input = jnp.einsum('gecr,grd->gecd', select, grouped, precision=lax.Precision.HIGHEST).astype(jnp.bfloat16)
    outputs = []
    for expert_index in range(EXP):
        expert_rows = slot_input[:, expert_index].reshape(GROUPS * CAP, D)
        columns = slice(expert_index * FF, (expert_index + 1) * FF)
        gate_value = jnp.dot(expert_rows, gate_all[:, columns], preferred_element_type=jnp.float32)
        up_value = jnp.dot(expert_rows, up_all[:, columns], preferred_element_type=jnp.float32)
        hidden = (jax.nn.silu(gate_value) * up_value).astype(jnp.bfloat16)
        produced = jnp.dot(hidden, down_all[columns, :], preferred_element_type=jnp.float32).astype(jnp.bfloat16)
        outputs.append(produced.reshape(GROUPS, CAP, D))
    slot_output = jnp.stack(outputs, axis=1)
    weight_table = jnp.transpose(route_weight.reshape(GROUPS, ROW_DEV, EXP), (0, 2, 1))
    coefficient = select * weight_table[:, :, None, :]
    expert_mix = jnp.einsum('gecr,gecd->grd', coefficient, slot_output.astype(jnp.float32), precision=lax.Precision.HIGHEST)
    expert_mix = expert_mix.reshape(ROWS, D).astype(jnp.bfloat16)
    finished = (stream + expert_mix.astype(jnp.float32)).astype(jnp.bfloat16)
    arranged = finished.reshape(PODS, N_DEV, ROW_DEV, D)
    blank = jnp.zeros((N_SIDE - PODS, N_DEV, ROW_DEV, D), jnp.bfloat16)
    return jnp.concatenate([arranged, blank], axis=0)
```

```python
import functools
import math

import jax
import jax.numpy as jnp
from jax import lax
from jax.experimental import pallas as pl
from jax.experimental.pallas import tpu as pltpu
from jax.sharding import PartitionSpec as P

MESH = pl.DeviceIdType.MESH
F32 = jnp.float32
BF16 = jnp.bfloat16

HD = 128
KVH = 8
GROUP = 4
EXP = 4
ROW = 8
CTX = 128
D = 4096
HALF = D // 2
QUARTER = D // 4
LANES = 128
WIDE = D + LANES
PAY = HALF + LANES
UNITS = 896
TILES = UNITS // LANES
CHUNKS = 3
LEFT, RIGHT = (0, HALF), (HALF, WIDE)
NEG = -1e30


def cols(start, stop):
    return pl.ds(start, stop - start)


def attention(q, nk, nv, ck, cv, lengths, res, gain, router, slot_rows, slot_count, kbuf, vbuf, stream, pay, sems):
    pieces = 4
    wide = KVH * HD // pieces

    def load(source, target, which, piece):
        span = pl.ds(piece * wide, wide)
        return pltpu.make_async_copy(source.at[:, :, span], target.at[:, :, span], sems.at[which, piece])

    for piece in range(pieces):
        load(ck, kbuf, 0, piece).start()
        load(cv, vbuf, 1, piece).start()
    scale = 1.0 / math.sqrt(HD)
    sub = lax.broadcasted_iota(jnp.int32, (ROW, LANES), 0)
    lane = lax.broadcasted_iota(jnp.int32, (ROW, LANES), 1)
    bias = jnp.concatenate(
        [jnp.where((sub == r) & (lane < lengths[0, 0, r]), 0.0, NEG) for r in range(ROW)], axis=1
    ).astype(F32)
    bias = jnp.concatenate([bias] * GROUP, axis=0)
    total = jnp.zeros((ROW, 1), F32)
    for k in range(KVH):
        if k % (KVH // pieces) == 0:
            load(ck, kbuf, 0, k // (KVH // pieces)).wait()
            load(cv, vbuf, 1, k // (KVH // pieces)).wait()
        span = slice(k * HD, (k + 1) * HD)
        heads = [slice((k * GROUP + g) * HD, (k * GROUP + g + 1) * HD) for g in range(GROUP)]
        query = jnp.concatenate([q[0, 0, :, h].astype(F32) for h in heads], axis=0)
        new_key = jnp.concatenate([nk[0, 0, :, span].astype(F32)] * GROUP, axis=0)
        new_value = jnp.concatenate([nv[0, 0, :, span].astype(F32)] * GROUP, axis=0)
        keys = kbuf[:, :, span].reshape(ROW * CTX, HD)
        values = vbuf[:, :, span].reshape(ROW * CTX, HD)
        scores = lax.dot_general(
            query.astype(BF16), keys, (((1,), (1,)), ((), ())), preferred_element_type=F32
        )
        scores = scores * scale + bias
        own = jnp.sum(query * new_key, axis=1, keepdims=True) * scale
        top = jnp.maximum(jnp.max(scores, axis=1, keepdims=True), own)
        probs = jnp.exp(scores - top)
        own_prob = jnp.exp(own - top)
        inverse = 1.0 / (jnp.sum(probs, axis=1, keepdims=True) + own_prob)
        weights = (probs * inverse).astype(BF16)
        own_weight = (own_prob * inverse).astype(BF16).astype(F32)
        context = jnp.dot(weights, values, preferred_element_type=F32) + own_weight * new_value
        for g, h in enumerate(heads):
            part = res[0, 0, :, h].astype(F32) + context[g * ROW : (g + 1) * ROW]
            stream[:, h] = part
            total = total + jnp.sum(part * part, axis=1, keepdims=True)
    rows = stream[...]
    normed = (rows * lax.rsqrt(total / D + 1e-05) * gain[...]).astype(BF16)
    logits = lax.dot_general(normed, router[...], (((1,), (1,)), ((), ())), preferred_element_type=F32)
    raised = []
    for e in range(EXP):
        chosen = jnp.zeros((ROW, 1), F32)
        for c in range(slot_rows.shape[3]):
            hit = (sub[:, 0:1] == slot_rows[0, 0, e, c]) & (c < slot_count[0, 0, e])
            chosen = chosen + jnp.where(hit, 1.0, 0.0)
        raised.append(chosen * jnp.exp(logits[:, e : e + 1]))
    inverse = raised[0] + raised[1] + raised[2] + raised[3]
    table = jnp.zeros((ROW, LANES), F32)
    for e in range(EXP):
        weight = raised[e] / inverse
        high = weight.astype(BF16).astype(F32)
        table = table + jnp.where(lane == e, high, 0.0) + jnp.where(lane == EXP + e, weight - high, 0.0)
    normed = normed.astype(F32)
    left = jnp.concatenate([normed[:, 0:HALF], table], axis=1)
    right = jnp.concatenate([normed[:, HALF:D], jnp.zeros((ROW, LANES), F32)], axis=1)
    pay[...] = jnp.concatenate([left, right], axis=0).astype(BF16)


def kernel(
    q, nk, nv, ck, cv, lengths, res, gain, router, gate, up, down, slot_rows, slot_count,
    out,
    kbuf, vbuf, stream, pay, arrived, back, fold,
    rows, parts, t1, t2, t3, t4, wide, wdown, hidden,
    kv_sems, w_sems, pay_send, pay_recv, g_send, g_recv, x_send, x_recv, p_send, p_recv, r_send, r_recv,
    b_send, b_recv,
):
    side, me = lax.axis_index("side"), lax.axis_index("dev")
    z, x, y = me // 16, lax.rem(me // 4, 4), lax.rem(me, 4)
    xp, x2, xm = (lax.rem(x + k, 4) for k in (1, 2, 3))
    yp, y2, ym = (lax.rem(y + k, 4) for k in (1, 2, 3))

    def at(z, x, y):
        return z * 16 + x * 4 + y

    near, far = at(1 - z, x, y), me
    barrier = pltpu.get_barrier_semaphore()

    def greet(side, dev):
        pl.semaphore_signal(barrier, inc=1, device_id={"side": side, "dev": dev}, device_id_type=MESH)

    def remote(src, dst, send, recv, side, dev):
        return pltpu.make_async_remote_copy(
            src_ref=src, dst_ref=dst, send_sem=send, recv_sem=recv,
            device_id={"side": side, "dev": dev}, device_id_type=MESH,
        )

    is_far_pod, is_hub, is_expert = side < 2, side == 2, side == 3

    @pl.when(is_far_pod)
    def _():
        greet(2, near)
        greet(2, far)

    @pl.when(is_hub)
    def _():
        for dev in (at(z, xp, y), at(z, xm, y), at(z, x, yp), at(z, x, ym), at(1 - z, x, y)):
            greet(2, dev)
        greet(3, me)
        for s in range(2):
            greet(s, near)
            greet(s, far)

    @pl.when(is_expert)
    def _():
        greet(2, me)

    def load_weights():
        copies = []
        for n in range(TILES):
            span = pl.ds(n * LANES, LANES)
            copies.append(
                pltpu.make_async_copy(gate.at[0, :, span], wide.at[n, :, pl.ds(0, LANES)], w_sems.at[0, n])
            )
            copies.append(
                pltpu.make_async_copy(up.at[0, :, span], wide.at[n, :, pl.ds(LANES, LANES)], w_sems.at[1, n])
            )
        copies.append(pltpu.make_async_copy(down.at[0], wdown, w_sems.at[2, 0]))
        return copies

    @pl.when(is_expert)
    def _():
        for copy in load_weights():
            copy.start()

    @pl.when(jnp.logical_not(is_expert))
    def _():
        attention(
            q, nk, nv, ck.at[0, 0], cv.at[0, 0], lengths, res, gain, router, slot_rows, slot_count,
            kbuf, vbuf, stream, pay, kv_sems,
        )

    pl.semaphore_wait(barrier, jnp.where(is_hub, 10, jnp.where(is_expert, 1, 2)))

    def unfold(block):
        return block[0:ROW], block[ROW : 2 * ROW]

    def finish():
        left0, right0 = unfold(back[0].astype(F32))
        left1, right1 = unfold(back[1].astype(F32))
        for start, mix in ((0, left0 + left1), (HALF, right0 + right1)):
            mix = mix.astype(BF16).astype(F32)
            out[0, 0, :, start : start + HALF] = (stream[:, start : start + HALF] + mix).astype(BF16)

    @pl.when(is_far_pod)
    def _():
        sent = [
            remote(pay, arrived.at[side], pay_send.at[0], pay_recv.at[side], 2, near),
            remote(pay, arrived.at[2 + side], pay_send.at[1], pay_recv.at[2 + side], 2, far),
        ]
        for copy in sent:
            copy.start()
        for copy in sent:
            copy.wait_send()
        for k in range(2):
            remote(back.at[k], back.at[k], b_send.at[0], b_recv.at[k], 2, me).wait_recv()
        finish()

    @pl.when(is_hub)
    def _():
        right_x, left_x = at(z, xp, y), at(z, xm, y)
        right_y, left_y = at(z, x, yp), at(z, x, ym)
        other = at(1 - z, x, y)
        started = []

        def go(copy):
            copy.start()
            started.append(copy)
            return copy

        trade = go(remote(pay, arrived.at[4], pay_send.at[0], pay_recv.at[4], 2, other))

        def take(slot):
            remote(arrived.at[slot], arrived.at[slot], pay_send.at[1], pay_recv.at[slot], 2, other).wait_recv()

        def pack(c):
            if c == 1:
                trade.wait_recv()
                first, second = pay[...].astype(F32), arrived[4].astype(F32)
            else:
                take(c)
                take(c + 1)
                first, second = arrived[c].astype(F32), arrived[c + 1].astype(F32)
            for begin, row, span in ((0, 0, (0, HALF)), (HALF, ROW, (0, HALF)), (D, 0, (HALF, PAY))):
                block = jnp.concatenate(
                    [first[row : row + ROW, span[0] : span[1]], second[row : row + ROW, span[0] : span[1]]],
                    axis=0,
                )
                rows[c, y, x, :, begin : begin + span[1] - span[0]] = block.astype(BF16)

        def ring(c, half, k, src, dst, dev):
            return go(remote(src, dst, g_send.at[c, half, k], g_recv.at[c, half, k], 2, dev))

        flights = {}

        def push(c, half, k, ref):
            go(remote(ref, ref, x_send.at[c, half, k], x_recv.at[c], 3, me))

        def line(c, half, j):
            begin, stop = (LEFT, RIGHT)[half]
            span = cols(begin, stop)
            return rows.at[c, j, :, :, span] if half == 0 else rows.at[c, :, j, :, span]

        def gather(c, step):
            for half in range(2):
                begin, stop = (LEFT, RIGHT)[half]
                whole, first, second = cols(begin, stop), cols(begin, begin + QUARTER), cols(begin + QUARTER, stop)
                along, across = ((x, xp, xm), (y, yp, ym))[:: 1 if half == 0 else -1]
                to_p, to_m = ((right_x, left_x), (right_y, left_y))[half]
                on_p, on_m = ((right_y, left_y), (right_x, left_x))[half]

                def slot(j, span):
                    return rows.at[c, y, j, :, span] if half == 0 else rows.at[c, j, x, :, span]

                def band(j, span):
                    return rows.at[c, j, :, :, span] if half == 0 else rows.at[c, :, j, :, span]

                key = (c, half)
                if step > 1:
                    for copy in flights[key]:
                        copy.wait_recv()
                if step == 1:
                    src = slot(along[0], whole)
                    flights[key] = [ring(c, half, 0, src, src, to_p), ring(c, half, 1, src, src, to_m)]
                elif step == 2:
                    a, b = slot(along[2], first), slot(along[1], second)
                    flights[key] = [ring(c, half, 2, a, a, to_p), ring(c, half, 3, b, b, to_m)]
                elif step == 3:
                    src = band(across[0], whole)
                    flights[key] = [ring(c, half, 4, src, src, on_p), ring(c, half, 5, src, src, on_m)]
                    push(c, half, 0, src)
                elif step == 4:
                    a, b = band(across[2], first), band(across[1], second)
                    flights[key] = [ring(c, half, 6, a, a, on_p), ring(c, half, 7, b, b, on_m)]
                    push(c, half, 1, band(across[1], whole))
                    push(c, half, 2, band(across[2], whole))
                else:
                    push(c, half, 3, band((y2, x2)[half], whole))

        sums = {}

        def leg(c, half, k, src, dst, dev):
            return go(remote(src, dst, r_send.at[c, half, k], r_recv.at[c, half, k], 2, dev))

        def reduce(c, step):
            for half in range(2):
                begin = half * HALF
                q0, q1 = (begin, begin + QUARTER), (begin + QUARTER, begin + HALF)
                whole = (begin, begin + HALF)
                across, along = ((y, yp, y2, ym), (x, xp, x2, xm))[:: 1 if half == 0 else -1]
                on_p, on_m = ((right_y, left_y), (right_x, left_x))[half]
                to_p, to_m = ((right_x, left_x), (right_y, left_y))[half]

                def slot(j, span):
                    span = cols(*span)
                    return parts.at[c, y, j, :, span] if half == 0 else parts.at[c, j, x, :, span]

                def band(j, span):
                    span = cols(*span)
                    return parts.at[c, j, :, :, span] if half == 0 else parts.at[c, :, j, :, span]

                def cell(j, i, span):
                    span = cols(*span)
                    return parts.at[c, j, i, :, span] if half == 0 else parts.at[c, i, j, :, span]

                key = (c, half)
                b1, b2, b3, b4 = t1.at[c, half], t2.at[c, half], t3.at[c, half], t4.at[c, half]
                if step == 1:
                    for quarter, span in enumerate((q0, q1)):
                        ref = parts.at[c, :, :, :, cols(*span)]
                        k = 2 * half + quarter
                        remote(ref, ref, p_send.at[c, k], p_recv.at[c, k], 3, me).wait_recv()
                    sums[key] = [
                        leg(c, half, 0, band(across[2], q0), b1.at[0], on_p),
                        leg(c, half, 1, band(across[2], q1), b1.at[1], on_m),
                    ]
                elif step == 2:
                    flying = []
                    for k, (j, span, dev) in enumerate(((across[1], q0, on_p), (across[3], q1, on_m))):
                        sums[key][k].wait_recv()
                        for i in range(4):
                            ref = cell(j, i, span)
                            ref[...] = (ref[...].astype(F32) + b1[k, i].astype(F32)).astype(BF16)
                        flying.append(leg(c, half, 2 + k, band(j, whole), b2.at[k], dev))
                    sums[key] = flying
                elif step == 3:
                    for copy in sums[key]:
                        copy.wait_recv()
                    for i in range(4):
                        ref = cell(across[0], i, whole)
                        ref[...] = (ref[...].astype(F32) + b2[0, i].astype(F32) + b2[1, i].astype(F32)).astype(BF16)
                    sums[key] = [
                        leg(c, half, 4, slot(along[2], q0), b3.at[0], to_p),
                        leg(c, half, 5, slot(along[2], q1), b3.at[1], to_m),
                    ]
                elif step == 4:
                    flying = []
                    for k, (j, span, dev) in enumerate(((along[1], q0, to_p), (along[3], q1, to_m))):
                        sums[key][k].wait_recv()
                        ref = slot(j, span)
                        ref[...] = (ref[...].astype(F32) + b3[k].astype(F32)).astype(BF16)
                        flying.append(leg(c, half, 6 + k, slot(j, whole), b4.at[k], dev))
                    sums[key] = flying
                else:
                    for copy in sums[key]:
                        copy.wait_recv()
                    ref = slot(along[0], whole)
                    block = ref[...].astype(F32) + b4[0].astype(F32) + b4[1].astype(F32)
                    sums[key] = block
            if step == 5:
                left, right = sums[(c, 0)], sums[(c, 1)]
                folded = [
                    jnp.concatenate([left[s * ROW : (s + 1) * ROW], right[s * ROW : (s + 1) * ROW]], axis=0)
                    for s in range(2)
                ]
                if c == 1:
                    back[0] = folded[0].astype(BF16)
                    fold[c, 1] = folded[1].astype(BF16)
                    sums["own"] = go(remote(fold.at[c, 1], back.at[1], b_send.at[c, 1], b_recv.at[1], 2, other))
                else:
                    for s in range(2):
                        fold[c, s] = folded[s].astype(BF16)
                        dev, k = (near, 0) if c == 0 else (far, 1)
                        go(remote(fold.at[c, s], back.at[k], b_send.at[c, s], b_recv.at[k], s, dev))

        pack(0)
        gather(0, 1)
        pack(1)
        gather(0, 2)
        gather(1, 1)
        pack(2)
        gather(0, 3)
        gather(1, 2)
        gather(2, 1)
        gather(0, 4)
        gather(1, 3)
        gather(2, 2)
        gather(0, 5)
        gather(1, 4)
        gather(2, 3)
        gather(1, 5)
        gather(2, 4)
        gather(2, 5)
        for c in range(CHUNKS):
            for step in range(1, 6):
                reduce(c, step)
        sums["own"].wait_recv()
        finish()
        for copy in started:
            copy.wait_send()

    @pl.when(is_expert)
    def _():
        expert = me // 8
        for copy in load_weights():
            copy.wait()
        lane = lax.broadcasted_iota(jnp.int32, (2 * LANES, LANES), 1)
        mine = (lane == expert) | (lane == expert + EXP)

        def send(c, k):
            ref = parts.at[c, :, :, :, pl.ds(k * QUARTER, QUARTER)]
            return remote(ref, ref, p_send.at[c, k], p_recv.at[c, k], 2, me)

        for c in range(CHUNKS):
            remote(rows.at[c], rows.at[c], x_send.at[c, 0, 0], x_recv.at[c], 2, me).wait_recv()
            table = rows[c, :, :, :, D:WIDE].reshape(2 * LANES, LANES).astype(F32)
            weight = jnp.sum(jnp.where(mine, table, 0.0), axis=1, keepdims=True)

            def units(n, carry):
                block = rows[c, :, :, :, 0:D].reshape(2 * LANES, D)
                both = jnp.dot(block, wide[n], preferred_element_type=F32)
                g, u = both[:, 0:LANES], both[:, LANES:]
                value = g * u / (1.0 + jnp.exp(-g)) * weight
                hidden[:, pl.ds(pl.multiple_of(n * LANES, LANES), LANES)] = value.astype(BF16)
                return carry

            lax.fori_loop(0, TILES, units, 0)
            for k in range(4):
                span = slice(k * QUARTER, (k + 1) * QUARTER)
                made = jnp.dot(hidden[...], wdown[:, span], preferred_element_type=F32)
                parts[c, :, :, :, span] = made.astype(BF16).reshape(4, 4, 2 * ROW, QUARTER)
                send(c, k).start()
        out[...] = jnp.zeros_like(out)
        for c in range(CHUNKS):
            for k in range(4):
                send(c, k).wait_send()


def local(
    query, new_key, new_value, cache_key, cache_value, lengths, residual,
    norm_gain, router_weight, gate_weight, up_weight, down_weight, slot_rows, slot_count,
):
    vmem, smem, hbm = (
        pl.BlockSpec(memory_space=pltpu.VMEM),
        pl.BlockSpec(memory_space=pltpu.SMEM),
        pl.BlockSpec(memory_space=pl.ANY),
    )
    dma = pltpu.SemaphoreType.DMA
    return pl.pallas_call(
        kernel,
        out_shape=jax.ShapeDtypeStruct(query.shape, BF16),
        in_specs=[vmem, vmem, vmem, hbm, hbm, smem, vmem, vmem, vmem, hbm, hbm, hbm, smem, smem],
        out_specs=vmem,
        scratch_shapes=[
            pltpu.VMEM((ROW, CTX, KVH * HD), BF16),
            pltpu.VMEM((ROW, CTX, KVH * HD), BF16),
            pltpu.VMEM((ROW, D), F32),
            pltpu.VMEM((2 * ROW, PAY), BF16),
            pltpu.VMEM((5, 2 * ROW, PAY), BF16),
            pltpu.VMEM((2, 2 * ROW, HALF), BF16),
            pltpu.VMEM((CHUNKS, 2, 2 * ROW, HALF), BF16),
            pltpu.VMEM((CHUNKS, 4, 4, 2 * ROW, WIDE), BF16),
            pltpu.VMEM((CHUNKS, 4, 4, 2 * ROW, D), BF16),
            pltpu.VMEM((CHUNKS, 2, 2, 4, 2 * ROW, QUARTER), BF16),
            pltpu.VMEM((CHUNKS, 2, 2, 4, 2 * ROW, HALF), BF16),
            pltpu.VMEM((CHUNKS, 2, 2, 2 * ROW, QUARTER), BF16),
            pltpu.VMEM((CHUNKS, 2, 2, 2 * ROW, HALF), BF16),
            pltpu.VMEM((TILES, D, 2 * LANES), BF16),
            pltpu.VMEM((UNITS, D), BF16),
            pltpu.VMEM((2 * LANES, UNITS), BF16),
            dma((2, 4)),
            dma((3, TILES)),
            dma((2,)),
            dma((5,)),
            dma((CHUNKS, 2, 8)),
            dma((CHUNKS, 2, 8)),
            dma((CHUNKS, 2, 4)),
            dma((CHUNKS,)),
            dma((CHUNKS, 4)),
            dma((CHUNKS, 4)),
            dma((CHUNKS, 2, 8)),
            dma((CHUNKS, 2, 8)),
            dma((CHUNKS, 2)),
            dma((2,)),
        ],
        compiler_params=pltpu.CompilerParams(
            collective_id=0, has_side_effects=True, vmem_limit_bytes=56 * 2**20
        ),
        name="moe_block",
    )(
        query, new_key, new_value, cache_key, cache_value, lengths, residual,
        norm_gain.reshape(1, D), jnp.transpose(router_weight),
        gate_weight, up_weight, down_weight, slot_rows, slot_count,
    )


def solution(mesh):
    return jax.shard_map(
        local,
        mesh=mesh,
        in_specs=(
            P("side", "dev", None, None),
            P("side", "dev", None, None),
            P("side", "dev", None, None),
            P("side", "dev", None, None, None),
            P("side", "dev", None, None, None),
            P("side", "dev", None),
            P("side", "dev", None, None),
            P(),
            P(),
            P("side", None, "dev"),
            P("side", None, "dev"),
            P("side", "dev", None),
            P("side", "dev", None, None),
            P("side", "dev", None),
        ),
        out_specs=P("side", "dev", None, None),
        check_vma=False,
    )
```

```python
import functools
import math

import jax
import jax.numpy as jnp
from jax import lax
from jax.experimental import pallas as pl
from jax.experimental.pallas import tpu as pltpu
from jax.sharding import PartitionSpec as P

MESH = pl.DeviceIdType.MESH
F32 = jnp.float32
BF16 = jnp.bfloat16

HD = 128
KVH = 8
GROUP = 4
EXP = 4
ROW = 8
CTX = 128
D = 4096
HALF = D // 2
QUARTER = D // 4
LANES = 128
WIDE = D + LANES
PAY = HALF + LANES
UNITS = 896
TILES = UNITS // LANES
CHUNKS = 3
LEFT, RIGHT = (0, HALF), (HALF, WIDE)
NEG = -1e30
ORDER = (0, 2, 1, 3)


def cols(start, stop):
    return pl.ds(start, stop - start)


def attention(q, nk, nv, ck, cv, lengths, res, gain, router, slot_rows, slot_count, kbuf, vbuf, stream, pay, sems):
    pieces = 4
    wide = KVH * HD // pieces

    def load(source, target, which, piece):
        span = pl.ds(piece * wide, wide)
        return pltpu.make_async_copy(source.at[:, :, span], target.at[:, :, span], sems.at[which, piece])

    for piece in range(pieces):
        load(ck, kbuf, 0, piece).start()
        load(cv, vbuf, 1, piece).start()
    scale = 1.0 / math.sqrt(HD)
    sub = lax.broadcasted_iota(jnp.int32, (ROW, LANES), 0)
    lane = lax.broadcasted_iota(jnp.int32, (ROW, LANES), 1)
    bias = jnp.concatenate(
        [jnp.where((sub == r) & (lane < lengths[0, 0, r]), 0.0, NEG) for r in range(ROW)], axis=1
    ).astype(F32)
    bias = jnp.concatenate([bias] * GROUP, axis=0)
    total = jnp.zeros((ROW, 1), F32)
    for k in range(KVH):
        if k % (KVH // pieces) == 0:
            load(ck, kbuf, 0, k // (KVH // pieces)).wait()
            load(cv, vbuf, 1, k // (KVH // pieces)).wait()
        span = slice(k * HD, (k + 1) * HD)
        heads = [slice((k * GROUP + g) * HD, (k * GROUP + g + 1) * HD) for g in range(GROUP)]
        query = jnp.concatenate([q[0, 0, :, h].astype(F32) for h in heads], axis=0)
        new_key = jnp.concatenate([nk[0, 0, :, span].astype(F32)] * GROUP, axis=0)
        new_value = jnp.concatenate([nv[0, 0, :, span].astype(F32)] * GROUP, axis=0)
        keys = kbuf[:, :, span].reshape(ROW * CTX, HD)
        values = vbuf[:, :, span].reshape(ROW * CTX, HD)
        scores = lax.dot_general(
            query.astype(BF16), keys, (((1,), (1,)), ((), ())), preferred_element_type=F32
        )
        scores = scores * scale + bias
        own = jnp.sum(query * new_key, axis=1, keepdims=True) * scale
        top = jnp.maximum(jnp.max(scores, axis=1, keepdims=True), own)
        probs = jnp.exp(scores - top)
        own_prob = jnp.exp(own - top)
        inverse = 1.0 / (jnp.sum(probs, axis=1, keepdims=True) + own_prob)
        weights = (probs * inverse).astype(BF16)
        own_weight = (own_prob * inverse).astype(BF16).astype(F32)
        context = jnp.dot(weights, values, preferred_element_type=F32) + own_weight * new_value
        for g, h in enumerate(heads):
            part = res[0, 0, :, h].astype(F32) + context[g * ROW : (g + 1) * ROW]
            stream[:, h] = part
            total = total + jnp.sum(part * part, axis=1, keepdims=True)
    rows = stream[...]
    normed = (rows * lax.rsqrt(total / D + 1e-05) * gain[...]).astype(BF16)
    logits = lax.dot_general(normed, router[...], (((1,), (1,)), ((), ())), preferred_element_type=F32)
    raised = []
    for e in range(EXP):
        chosen = jnp.zeros((ROW, 1), F32)
        for c in range(slot_rows.shape[3]):
            hit = (sub[:, 0:1] == slot_rows[0, 0, e, c]) & (c < slot_count[0, 0, e])
            chosen = chosen + jnp.where(hit, 1.0, 0.0)
        raised.append(chosen * jnp.exp(logits[:, e : e + 1]))
    inverse = raised[0] + raised[1] + raised[2] + raised[3]
    table = jnp.zeros((ROW, LANES), F32)
    for e in range(EXP):
        weight = raised[e] / inverse
        high = weight.astype(BF16).astype(F32)
        table = table + jnp.where(lane == e, high, 0.0) + jnp.where(lane == EXP + e, weight - high, 0.0)
    normed = normed.astype(F32)
    left = jnp.concatenate([normed[:, 0:HALF], table], axis=1)
    right = jnp.concatenate([normed[:, HALF:D], jnp.zeros((ROW, LANES), F32)], axis=1)
    pay[...] = jnp.concatenate([left, right], axis=0).astype(BF16)


def kernel(
    q, nk, nv, ck, cv, lengths, res, gain, router, gate, up, down, slot_rows, slot_count,
    out,
    kbuf, vbuf, stream, pay, arrived, back, fold,
    rows, parts, landed, merged, crossed, wide, wdown, hidden,
    kv_sems, w_sems, pay_send, pay_recv, g_send, g_recv, p_send, p_recv, r_send, r_recv, b_send, b_recv,
):
    side, me = lax.axis_index("side"), lax.axis_index("dev")
    z, x, y = me // 16, lax.rem(me // 4, 4), lax.rem(me, 4)
    xs = [x] + [lax.rem(x + k, 4) for k in (1, 2, 3)]
    ys = [y] + [lax.rem(y + k, 4) for k in (1, 2, 3)]

    def at(z, x, y):
        return z * 16 + x * 4 + y

    near, far = at(1 - z, x, y), me
    in_line = [at(z, xs[k], y) for k in (1, 2, 3)] + [at(z, x, ys[k]) for k in (1, 2, 3)]
    barrier = pltpu.get_barrier_semaphore()

    def greet(side, dev):
        pl.semaphore_signal(barrier, inc=1, device_id={"side": side, "dev": dev}, device_id_type=MESH)

    def remote(src, dst, send, recv, side, dev):
        return pltpu.make_async_remote_copy(
            src_ref=src, dst_ref=dst, send_sem=send, recv_sem=recv,
            device_id={"side": side, "dev": dev}, device_id_type=MESH,
        )

    is_far_pod, is_hub, is_expert = side < 2, side == 2, side == 3

    @pl.when(is_far_pod)
    def _():
        for s in (2, 3):
            greet(s, near)
            greet(s, far)

    @pl.when(jnp.logical_not(is_far_pod))
    def _():
        for s in (2, 3):
            for dev in in_line:
                greet(s, dev)
        greet(5 - side, me)
        greet(5 - side, near)
        for s in (0, 1):
            greet(s, near)
            greet(s, far)

    @pl.when(is_hub)
    def _():
        greet(2, near)

    def load_weights():
        copies = []
        for n in range(TILES):
            span = pl.ds(n * LANES, LANES)
            copies.append(
                pltpu.make_async_copy(gate.at[0, :, span], wide.at[n, :, pl.ds(0, LANES)], w_sems.at[0, n])
            )
            copies.append(
                pltpu.make_async_copy(up.at[0, :, span], wide.at[n, :, pl.ds(LANES, LANES)], w_sems.at[1, n])
            )
        copies.append(pltpu.make_async_copy(down.at[0], wdown, w_sems.at[2, 0]))
        return copies

    @pl.when(is_expert)
    def _():
        for copy in load_weights():
            copy.start()

    @pl.when(jnp.logical_not(is_expert))
    def _():
        attention(
            q, nk, nv, ck.at[0, 0], cv.at[0, 0], lengths, res, gain, router, slot_rows, slot_count,
            kbuf, vbuf, stream, pay, kv_sems,
        )

    pl.semaphore_wait(barrier, jnp.where(is_hub, 19, jnp.where(is_expert, 18, 4)))

    def unfold(block):
        return block[0:ROW], block[ROW : 2 * ROW]

    def finish():
        left0, right0 = unfold(back[0].astype(F32))
        left1, right1 = unfold(back[1].astype(F32))
        for start, mix in ((0, left0 + left1), (HALF, right0 + right1)):
            mix = mix.astype(BF16).astype(F32)
            out[0, 0, :, start : start + HALF] = (stream[:, start : start + HALF] + mix).astype(BF16)

    @pl.when(is_far_pod)
    def _():
        sent = [
            remote(pay, arrived.at[side], pay_send.at[0], pay_recv.at[side], 3, near),
            remote(pay, arrived.at[2 + side], pay_send.at[1], pay_recv.at[2 + side], 3, far),
        ]
        for copy in sent:
            copy.start()
        for copy in sent:
            copy.wait_send()
        for k in range(2):
            remote(back.at[k], back.at[k], b_send.at[0, 0], b_recv.at[k], 2, me).wait_recv()
        finish()

    @pl.when(is_hub)
    def _():
        started = []

        def go(copy):
            copy.start()
            started.append(copy)
            return copy

        go(remote(pay, arrived.at[4], pay_send.at[0], pay_recv.at[4], 3, me))
        go(remote(pay, arrived.at[5], pay_send.at[1], pay_recv.at[5], 3, near))
        flights = {}

        def first(c, u):
            for k in range(4):
                ref = landed.at[c, u, k]
                remote(ref, ref, p_send.at[c, u, k], p_recv.at[c, u, k], 3, me).wait_recv()
            for i in range(4):
                total = landed[c, u, 0, i].astype(F32)
                for k in range(1, 4):
                    total = total + landed[c, u, k, i].astype(F32)
                merged[c, u, i] = total.astype(BF16)
            flights[c, u] = []
            for k in range(1, 4):
                j, dev = (xs[k], at(z, xs[k], y)) if u < 2 else (ys[k], at(z, x, ys[k]))
                flights[c, u].append(
                    go(remote(merged.at[c, u, j], crossed.at[c, u, k - 1], r_send.at[c, u, k - 1], r_recv.at[c, u, k - 1], 2, dev))
                )

        def second(c, u):
            for copy in flights[c, u]:
                copy.wait_recv()
            total = merged[c, u, x if u < 2 else y].astype(F32)
            for k in range(3):
                total = total + crossed[c, u, k].astype(F32)
            return total

        def give(c, sums):
            halves = [jnp.concatenate(sums[0:2], axis=1), jnp.concatenate(sums[2:4], axis=1)]
            folded = [
                jnp.concatenate([half[s * ROW : (s + 1) * ROW] for half in halves], axis=0).astype(BF16)
                for s in range(2)
            ]
            if c == 0:
                back[0] = folded[0]
                fold[c, 1] = folded[1]
                flights["own"] = go(remote(fold.at[c, 1], back.at[1], b_send.at[c, 1], b_recv.at[1], 2, near))
            else:
                for s in range(2):
                    fold[c, s] = folded[s]
                    dev, k = (far, 1) if c == 1 else (near, 0)
                    go(remote(fold.at[c, s], back.at[k], b_send.at[c, s], b_recv.at[k], s, dev))

        for c in range(CHUNKS):
            for u in ORDER:
                first(c, u)
            sums = [second(c, u) for u in range(4)]
            give(c, sums)
        flights["own"].wait_recv()
        finish()
        for copy in started:
            copy.wait_send()

    @pl.when(is_expert)
    def _():
        expert = me // 8
        started = []

        def go(copy):
            copy.start()
            started.append(copy)
            return copy

        def pack(c):
            slots = ((4, 5), (2, 3), (0, 1))[c]
            for slot in slots:
                remote(arrived.at[slot], arrived.at[slot], pay_send.at[0], pay_recv.at[slot], 2, me).wait_recv()
            a, b = (arrived[slot].astype(F32) for slot in slots)
            for begin, row, span in ((0, 0, (0, HALF)), (HALF, ROW, (0, HALF)), (D, 0, (HALF, PAY))):
                block = jnp.concatenate(
                    [a[row : row + ROW, span[0] : span[1]], b[row : row + ROW, span[0] : span[1]]], axis=0
                )
                rows[c, y, x, :, begin : begin + span[1] - span[0]] = block.astype(BF16)

        flights = {}

        def spread(c, phase):
            made = []
            for half in range(2):
                span = cols(*(LEFT, RIGHT)[half])
                for k in (1, 2, 3):
                    on_x = at(z, xs[k], y)
                    on_y = at(z, x, ys[k])
                    if phase == 0:
                        ref, dev = rows.at[c, y, x, :, span], (on_x, on_y)[half]
                    elif half == 0:
                        ref, dev = rows.at[c, y, :, :, span], on_y
                    else:
                        ref, dev = rows.at[c, :, x, :, span], on_x
                    made.append(
                        go(remote(ref, ref, g_send.at[c, phase, half, k - 1], g_recv.at[c, phase, half, k - 1], 3, dev))
                    )
            flights[c, phase] = made

        def gathered(c, phase):
            for copy in flights[c, phase]:
                copy.wait_recv()

        pack(0)
        spread(0, 0)
        pack(2)
        spread(2, 0)
        pack(1)
        spread(1, 0)
        for c in range(CHUNKS):
            gathered(c, 0)
            spread(c, 1)
        for copy in load_weights():
            copy.wait()
        lane = lax.broadcasted_iota(jnp.int32, (2 * LANES, LANES), 1)
        mine = (lane == expert) | (lane == expert + EXP)
        for c in range(CHUNKS):
            gathered(c, 1)
            table = rows[c, :, :, :, D:WIDE].reshape(2 * LANES, LANES).astype(F32)
            weight = jnp.sum(jnp.where(mine, table, 0.0), axis=1, keepdims=True)

            def units(n, carry):
                block = rows[c, :, :, :, 0:D].reshape(2 * LANES, D)
                both = jnp.dot(block, wide[n], preferred_element_type=F32)
                g, u = both[:, 0:LANES], both[:, LANES:]
                value = g * u / (1.0 + jnp.exp(-g)) * weight
                hidden[:, pl.ds(pl.multiple_of(n * LANES, LANES), LANES)] = value.astype(BF16)
                return carry

            lax.fori_loop(0, TILES, units, 0)
            for u in ORDER:
                span = slice(u * QUARTER, (u + 1) * QUARTER)
                made = jnp.dot(hidden[...], wdown[:, span], preferred_element_type=F32)
                parts[c, :, :, :, span] = made.astype(BF16).reshape(4, 4, 2 * ROW, QUARTER)
                for k in range(4):
                    if u < 2:
                        src, dev = parts.at[c, ys[k], :, :, cols(u * QUARTER, (u + 1) * QUARTER)], at(z, x, ys[k])
                    else:
                        src, dev = parts.at[c, :, xs[k], :, cols(u * QUARTER, (u + 1) * QUARTER)], at(z, xs[k], y)
                    go(remote(src, landed.at[c, u, k], p_send.at[c, u, k], p_recv.at[c, u, k], 2, dev))
        out[...] = jnp.zeros_like(out)
        for copy in started:
            copy.wait_send()


def local(
    query, new_key, new_value, cache_key, cache_value, lengths, residual,
    norm_gain, router_weight, gate_weight, up_weight, down_weight, slot_rows, slot_count,
):
    vmem, smem, hbm = (
        pl.BlockSpec(memory_space=pltpu.VMEM),
        pl.BlockSpec(memory_space=pltpu.SMEM),
        pl.BlockSpec(memory_space=pl.ANY),
    )
    dma = pltpu.SemaphoreType.DMA
    return pl.pallas_call(
        kernel,
        out_shape=jax.ShapeDtypeStruct(query.shape, BF16),
        in_specs=[vmem, vmem, vmem, hbm, hbm, smem, vmem, vmem, vmem, hbm, hbm, hbm, smem, smem],
        out_specs=vmem,
        scratch_shapes=[
            pltpu.VMEM((ROW, CTX, KVH * HD), BF16),
            pltpu.VMEM((ROW, CTX, KVH * HD), BF16),
            pltpu.VMEM((ROW, D), F32),
            pltpu.VMEM((2 * ROW, PAY), BF16),
            pltpu.VMEM((6, 2 * ROW, PAY), BF16),
            pltpu.VMEM((2, 2 * ROW, HALF), BF16),
            pltpu.VMEM((CHUNKS, 2, 2 * ROW, HALF), BF16),
            pltpu.VMEM((CHUNKS, 4, 4, 2 * ROW, WIDE), BF16),
            pltpu.VMEM((CHUNKS, 4, 4, 2 * ROW, D), BF16),
            pltpu.VMEM((CHUNKS, 4, 4, 4, 2 * ROW, QUARTER), BF16),
            pltpu.VMEM((CHUNKS, 4, 4, 2 * ROW, QUARTER), BF16),
            pltpu.VMEM((CHUNKS, 4, 3, 2 * ROW, QUARTER), BF16),
            pltpu.VMEM((TILES, D, 2 * LANES), BF16),
            pltpu.VMEM((UNITS, D), BF16),
            pltpu.VMEM((2 * LANES, UNITS), BF16),
            dma((2, 4)),
            dma((3, TILES)),
            dma((2,)),
            dma((6,)),
            dma((CHUNKS, 2, 2, 3)),
            dma((CHUNKS, 2, 2, 3)),
            dma((CHUNKS, 4, 4)),
            dma((CHUNKS, 4, 4)),
            dma((CHUNKS, 4, 3)),
            dma((CHUNKS, 4, 3)),
            dma((CHUNKS, 2)),
            dma((2,)),
        ],
        compiler_params=pltpu.CompilerParams(
            collective_id=0, has_side_effects=True, vmem_limit_bytes=56 * 2**20
        ),
        name="moe_block",
    )(
        query, new_key, new_value, cache_key, cache_value, lengths, residual,
        norm_gain.reshape(1, D), jnp.transpose(router_weight),
        gate_weight, up_weight, down_weight, slot_rows, slot_count,
    )


def solution(mesh):
    return jax.shard_map(
        local,
        mesh=mesh,
        in_specs=(
            P("side", "dev", None, None),
            P("side", "dev", None, None),
            P("side", "dev", None, None),
            P("side", "dev", None, None, None),
            P("side", "dev", None, None, None),
            P("side", "dev", None),
            P("side", "dev", None, None),
            P(),
            P(),
            P("side", None, "dev"),
            P("side", None, "dev"),
            P("side", "dev", None),
            P("side", "dev", None, None),
            P("side", "dev", None),
        ),
        out_specs=P("side", "dev", None, None),
        check_vma=False,
    )
```

```python
import functools
import math

import jax
import jax.numpy as jnp
from jax import lax
from jax.experimental import pallas as pl
from jax.experimental.pallas import tpu as pltpu
from jax.sharding import PartitionSpec as P

MESH = pl.DeviceIdType.MESH
F32 = jnp.float32
BF16 = jnp.bfloat16

HD = 128
KVH = 8
GROUP = 4
EXP = 4
ROW = 8
CTX = 128
D = 4096
HALF = D // 2
QUARTER = D // 4
LANES = 128
FOLD = HALF + LANES
UNITS = 896
TILES = UNITS // LANES
CHUNKS = 6
SPANS = ((0, QUARTER), (QUARTER, FOLD))
BATCH = 16 * ROW
FIRST, SECOND, LAST = 0, 1, CHUNKS - 1
DIRECT = 5
NEG = -1e30


def cols(start, stop):
    return pl.ds(start, stop - start)


def attention(q, nk, nv, ck, cv, lengths, res, gain, router, slot_rows, slot_count, kbuf, vbuf, stream, pay, sems):
    pieces = 2
    wide = KVH * HD // pieces

    def load(source, target, which, piece):
        span = pl.ds(piece * wide, wide)
        return pltpu.make_async_copy(source.at[:, :, span], target.at[:, :, span], sems.at[which, piece])

    for piece in range(pieces):
        load(ck, kbuf, 0, piece).start()
        load(cv, vbuf, 1, piece).start()
    scale = 1.0 / math.sqrt(HD)
    sub = lax.broadcasted_iota(jnp.int32, (ROW, LANES), 0)
    lane = lax.broadcasted_iota(jnp.int32, (ROW, LANES), 1)
    length = jnp.zeros((ROW, LANES), jnp.int32)
    for r in range(ROW):
        length = jnp.where(sub == r, lengths[0, 0, r], length)
    seen = jnp.concatenate([lane < length] * GROUP, axis=0)
    row = jnp.concatenate([sub] * GROUP, axis=0)
    spans = [slice(k * HD, (k + 1) * HD) for k in range(KVH)]
    scores, own, new_values = [], [], []
    for k, span in enumerate(spans):
        if k % (KVH // pieces) == 0:
            load(ck, kbuf, 0, k // (KVH // pieces)).wait()
        heads = [slice((k * GROUP + g) * HD, (k * GROUP + g + 1) * HD) for g in range(GROUP)]
        query = jnp.concatenate([q[0, 0, :, h].astype(F32) for h in heads], axis=0)
        new_key = jnp.concatenate([nk[0, 0, :, span].astype(F32)] * GROUP, axis=0)
        new_values.append(jnp.concatenate([nv[0, 0, :, span].astype(F32)] * GROUP, axis=0))
        keys = kbuf[:, :, span].reshape(ROW * CTX, HD)
        every = lax.dot_general(query.astype(BF16), keys, (((1,), (1,)), ((), ())), preferred_element_type=F32)
        kept = every[:, 0:CTX]
        for r in range(1, ROW):
            kept = jnp.where(row == r, every[:, r * CTX : (r + 1) * CTX], kept)
        scores.append(jnp.where(seen, kept * scale, NEG))
        own.append(jnp.sum(query * new_key, axis=1, keepdims=True) * scale)
    weights, own_weights = [], []
    for k in range(KVH):
        top = jnp.maximum(jnp.max(scores[k], axis=1, keepdims=True), own[k])
        probs = jnp.exp(scores[k] - top)
        own_prob = jnp.exp(own[k] - top)
        inverse = 1.0 / (jnp.sum(probs, axis=1, keepdims=True) + own_prob)
        weights.append(probs * inverse)
        own_weights.append((own_prob * inverse).astype(BF16).astype(F32))
    total = jnp.zeros((ROW, LANES), F32)
    for k, span in enumerate(spans):
        if k % (KVH // pieces) == 0:
            load(cv, vbuf, 1, k // (KVH // pieces)).wait()
        values = vbuf[:, :, span].reshape(ROW * CTX, HD)
        spaced = jnp.concatenate([jnp.where(row == r, weights[k], 0.0).astype(BF16) for r in range(ROW)], axis=1)
        context = jnp.dot(spaced, values, preferred_element_type=F32) + own_weights[k] * new_values[k]
        for g in range(GROUP):
            h = slice((k * GROUP + g) * HD, (k * GROUP + g + 1) * HD)
            part = res[0, 0, :, h].astype(F32) + context[g * ROW : (g + 1) * ROW]
            stream[:, h] = part
            total = total + part * part
    total = jnp.sum(total, axis=1, keepdims=True)
    rows = stream[...]
    normed = (rows * lax.rsqrt(total / D + 1e-05) * gain[...]).astype(BF16)
    logits = lax.dot_general(normed, router[...], (((1,), (1,)), ((), ())), preferred_element_type=F32)
    raised = []
    for e in range(EXP):
        chosen = jnp.zeros((ROW, 1), F32)
        for c in range(slot_rows.shape[3]):
            hit = (sub[:, 0:1] == slot_rows[0, 0, e, c]) & (c < slot_count[0, 0, e])
            chosen = chosen + jnp.where(hit, 1.0, 0.0)
        raised.append(chosen * jnp.exp(logits[:, e : e + 1]))
    inverse = raised[0] + raised[1] + raised[2] + raised[3]
    table = jnp.zeros((ROW, LANES), F32)
    for e in range(EXP):
        weight = raised[e] / inverse
        high = weight.astype(BF16).astype(F32)
        table = table + jnp.where(lane == e, high, 0.0) + jnp.where(lane == EXP + e, weight - high, 0.0)
    normed = normed.astype(F32)
    upper = [normed[:, 0:QUARTER], normed[:, HALF : HALF + QUARTER], table]
    lower = [normed[:, QUARTER:HALF], normed[:, HALF + QUARTER : D], jnp.zeros((ROW, LANES), F32)]
    pay[...] = jnp.concatenate([jnp.concatenate(upper, axis=1), jnp.concatenate(lower, axis=1)], axis=0).astype(BF16)


def kernel(
    q, nk, nv, ck, cv, lengths, res, gain, router, gate, up, down, slot_rows, slot_count,
    out,
    kbuf, vbuf, stream, pay, back, done,
    rows, parts, turned, passed, merged, crossed, wide, wdown, block, weight, hidden,
    kv_sems, w_sems, pay_send, pay_recv, g_send, g_recv, p_send, p_recv, own_recv, r_send, r_recv, b_send, b_recv,
):
    side, me = lax.axis_index("side"), lax.axis_index("dev")
    z, x, y = me // 16, lax.rem(me // 4, 4), lax.rem(me, 4)
    xs = [x] + [lax.rem(x + k, 4) for k in (1, 2, 3)]
    ys = [y] + [lax.rem(y + k, 4) for k in (1, 2, 3)]

    def at(z, x, y):
        return z * 16 + x * 4 + y

    near, far = at(1 - z, x, y), me
    in_line = [at(z, xs[k], y) for k in (1, 2, 3)] + [at(z, x, ys[k]) for k in (1, 2, 3)]
    barrier = pltpu.get_barrier_semaphore()

    def greet(side, dev):
        pl.semaphore_signal(barrier, inc=1, device_id={"side": side, "dev": dev}, device_id_type=MESH)

    def remote(src, dst, send, recv, side, dev):
        return pltpu.make_async_remote_copy(
            src_ref=src, dst_ref=dst, send_sem=send, recv_sem=recv,
            device_id={"side": side, "dev": dev}, device_id_type=MESH,
        )

    is_far_pod, is_hub, is_expert = side < 2, side == 2, side == 3

    @pl.when(is_far_pod)
    def _():
        for s in (2, 3):
            greet(s, near)
            greet(s, far)
        for dev in in_line:
            greet(side, dev)

    @pl.when(jnp.logical_not(is_far_pod))
    def _():
        for s in (2, 3):
            for dev in in_line:
                greet(s, dev)
        greet(5 - side, me)
        greet(5 - side, near)
        for s in (0, 1):
            greet(s, near)
            greet(s, far)

    @pl.when(is_hub)
    def _():
        greet(2, near)

    def load_weights():
        for n in range(TILES):
            span = pl.ds(n * LANES, LANES)
            pltpu.make_async_copy(gate.at[0, :, span], wide.at[n, :, pl.ds(0, LANES)], w_sems.at[0]).start()
            pltpu.make_async_copy(up.at[0, :, span], wide.at[n, :, pl.ds(LANES, LANES)], w_sems.at[0]).start()
        pltpu.make_async_copy(down.at[0], wdown, w_sems.at[1]).start()

    @pl.when(is_expert)
    def _():
        load_weights()

    @pl.when(jnp.logical_not(is_expert))
    def _():
        attention(
            q, nk, nv, ck.at[0, 0], cv.at[0, 0], lengths, res, gain, router, slot_rows, slot_count,
            kbuf, vbuf, stream, pay, kv_sems,
        )

    pl.semaphore_wait(barrier, jnp.where(is_hub, 19, jnp.where(is_expert, 18, 10)))

    def finish():
        for h in range(2):
            mix = back[0, h].astype(F32) + back[1, h].astype(F32)
            for k in range(2):
                span = slice((2 * h + k) * QUARTER, (2 * h + k + 1) * QUARTER)
                part = mix[k * ROW : (k + 1) * ROW].astype(BF16).astype(F32)
                out[0, 0, :, span] = (stream[:, span] + part).astype(BF16)

    def arrived(ref, sem):
        remote(ref, ref, pay_send.at[0], sem, side, me).wait_recv()

    def sent(ref, sem):
        remote(ref, ref, sem, pay_recv.at[0], side, me).wait_send()

    def give_rows(c, dev):
        remote(pay, rows.at[c, y, x], pay_send.at[0], pay_recv.at[c], 3, dev).start()

    here = (ys, xs)
    line_devs = ([at(z, x, ys[k]) for k in range(4)], [at(z, xs[k], y) for k in range(4)])

    def band(ref, h, j, span=slice(None)):
        return ref.at[j, :, :, span] if h == 0 else ref.at[:, j, :, span]

    def spread(c, phase, straight):
        for h in range(2):
            begin, stop = SPANS[h]
            whole = cols(begin, stop)
            halves = cols(begin, begin + QUARTER // 2), cols(begin + QUARTER // 2, stop)

            def send(ref, which, dev):
                remote(ref, ref, g_send.at[which], g_recv.at[c, phase], side, dev).start()

            if phase == 0:
                for k in (1, 2, 3):
                    send(rows.at[c, y, x, :, whole], 0, line_devs[1 - h][k])
            elif phase == 1:
                for k in (1, 3, 2) if straight else (1, 3):
                    send(band(rows.at[c], h, here[h][0], whole), 2 if straight else 1, line_devs[h][k])
            else:
                send(band(rows.at[c], h, here[h][3], halves[0]), 1, line_devs[h][1])
                send(band(rows.at[c], h, here[h][1], halves[1]), 1, line_devs[h][3])

    def landed(c, phase, straight):
        ref = rows.at[c, 0, 0:3] if phase == 0 else rows.at[c, 0 : 3 if straight else 3 - phase]
        arrived(ref, g_recv.at[c, phase])

    @pl.when(is_far_pod)
    def _():
        @pl.when(side == 1)
        def _():
            give_rows(LAST - 1, near)
            give_rows(3, far)
            sent(rows.at[0, 0, 0:2], pay_send.at[0])

        @pl.when(side == 0)
        def _():
            rows[LAST, y, x] = pay[...]
            spread(LAST, 0, True)
            give_rows(2, far)
            landed(LAST, 0, True)
            spread(LAST, 1, True)

            def push(k):
                for h in range(2):
                    ref = band(rows.at[LAST], h, here[h][k], cols(*SPANS[h]))
                    remote(ref, ref, p_send.at[0], g_recv.at[LAST, 2], 3, near).start()

            push(0)
            landed(LAST, 1, True)
            for k in (1, 3, 2):
                push(k)
            sent(rows.at[0, 0, 0:1], pay_send.at[0])
            sent(rows.at[LAST, 0, 0:3], g_send.at[0])
            sent(rows.at[LAST, 0:3], g_send.at[2])
            sent(rows.at[LAST], p_send.at[0])

        arrived(back, b_recv.at[0])
        finish()

    @pl.when(is_hub)
    def _():
        give_rows(0, me)
        give_rows(1, near)

        def cell(c, h, j, i):
            return parts.at[c, h, j, i] if h == 0 else parts.at[c, h, i, j]

        def first(c, h):
            arrived(parts.at[c, h], own_recv.at[c, h])
            arrived(turned.at[c, h], p_recv.at[c, h])
            if c == CHUNKS - 1:
                return
            for k, step in enumerate((1, 3)):
                span = slice(k * QUARTER // 2, (k + 1) * QUARTER // 2)
                for i in range(4):
                    ref = cell(c, h, here[h][step], i).at[:, span]
                    ref[...] = (ref[...].astype(F32) + turned[c, h, k, i].astype(F32)).astype(BF16)
                src = band(parts.at[c, h], h, here[h][step])
                remote(src, passed.at[c, h, k], r_send.at[0], r_recv.at[c, h], 2, line_devs[h][step]).start()

        def middle(c, h):
            arrived(passed.at[c, h], r_recv.at[c, h])
            for i in range(4):
                total = cell(c, h, here[h][0], i)[...].astype(F32) + passed[c, h, 0, i].astype(F32)
                total = total + passed[c, h, 1, i].astype(F32)
                if c == CHUNKS - 1:
                    halves = [turned[c, h, k, i].astype(F32) for k in range(2)]
                    total = total + jnp.concatenate(halves, axis=1)
                merged[c, h, i] = total.astype(BF16)
            for k in range(1, 4):
                src, dst = merged.at[c, h, here[1 - h][k]], crossed.at[c, h, k - 1]
                remote(src, dst, r_send.at[1], r_recv.at[c, 2], 2, line_devs[1 - h][k]).start()

        def second(c):
            target = back.at[0] if c == 0 else done.at[c]
            arrived(crossed.at[c], r_recv.at[c, 2])
            for h in range(2):
                total = merged[c, h, here[1 - h][0]].astype(F32)
                for k in range(3):
                    total = total + crossed[c, h, k].astype(F32)
                target[h] = total.astype(BF16)
            if c > 0:
                side, dev, k = ((2, near, 1), (0, far, 1), (1, far, 1), (1, near, 0), (0, near, 0))[c - 1]
                remote(done.at[c], back.at[k], b_send.at[0], b_recv.at[0], side, dev).start()

        def both(step, c):
            for h in range(2):
                step(c, h)

        for c in range(CHUNKS):
            if c < LAST:
                both(first, c)
            if c > 0:
                both(middle, c - 1)
            if c > 1:
                second(c - 2)
        both(first, LAST)
        both(middle, LAST)
        second(LAST - 1)
        second(LAST)
        arrived(back.at[1], b_recv.at[0])
        finish()
        sent(rows.at[0, 0, 0:2], pay_send.at[0])
        sent(passed.at[0 : CHUNKS - 1], r_send.at[0])
        sent(crossed, r_send.at[1])
        sent(done.at[1:CHUNKS], b_send.at[0])

    @pl.when(is_expert)
    def _():
        expert = me // 8

        def is_last(c):
            return isinstance(c, int) and c == LAST

        def widen(c, phase, straight=False):
            landed(c, phase - 1, straight)
            spread(c, phase, straight)

        def share(c, h):
            ref = parts.at[c, h]
            for k, step in enumerate((1, 3)):
                span = pl.ds(k * QUARTER // 2, QUARTER // 2)
                dev = line_devs[h][2 if is_last(c) else step]
                remote(band(ref, h, here[h][2], span), turned.at[c, h, k], p_send.at[0], p_recv.at[c, h], 2, dev).start()
                if is_last(c):
                    src = band(ref, h, here[h][step])
                    remote(src, passed.at[c, h, 1 - k], p_send.at[2], r_recv.at[c, h], 2, line_devs[h][step]).start()
            remote(ref, ref, p_send.at[1], own_recv.at[c, h], 2, me).start()

        for c in range(DIRECT):
            arrived(rows.at[c, y, x], pay_recv.at[c])
            spread(c, 0, False)
        widen(FIRST, 1, True)
        sent(rows.at[FIRST, 0:3], g_send.at[2])
        widen(SECOND, 1, True)
        widen(2, 1)
        pltpu.make_async_copy(wide, wide, w_sems.at[0]).wait()
        pltpu.make_async_copy(wdown, wdown, w_sems.at[1]).wait()
        lane = lax.broadcasted_iota(jnp.int32, (ROW, LANES), 1)
        mine = (lane == expert) | (lane == expert + EXP)

        def unfold(c):
            for i in range(8):
                pair = [rows[c, i // 2, 2 * (i % 2) + k].astype(F32) for k in range(2)]
                to = slice(i * 2 * ROW, (i + 1) * 2 * ROW)
                for k in range(4):
                    row, begin = (k % 2) * ROW, (k // 2) * QUARTER
                    piece = [p[row : row + ROW, begin : begin + QUARTER] for p in pair]
                    block[to, k * QUARTER : (k + 1) * QUARTER] = jnp.concatenate(piece, axis=0).astype(BF16)
                table = [jnp.where(mine, p[0:ROW, HALF:FOLD], 0.0) for p in pair]
                table = [jnp.broadcast_to(jnp.sum(t, axis=1, keepdims=True), (ROW, LANES)) for t in table]
                weight[to, :] = jnp.concatenate(table, axis=0)

        def lift():
            for n in range(TILES):
                both = jnp.dot(block[...], wide[n], preferred_element_type=F32)
                g, u = both[:, 0:LANES], both[:, LANES:]
                hidden[:, n * LANES : (n + 1) * LANES] = (g * u / (1.0 + jnp.exp(-g)) * weight[...]).astype(BF16)

        def lower(c, h):
            made = jnp.dot(hidden[...], wdown[:, h * HALF : (h + 1) * HALF], preferred_element_type=F32)
            made = made.reshape(16, ROW, HALF)
            made = jnp.concatenate([made[:, :, 0:QUARTER], made[:, :, QUARTER:HALF]], axis=1)
            parts[c, h] = made.astype(BF16).reshape(4, 4, 2 * ROW, QUARTER)

        def batch(c, carry):
            lift()

            @pl.when(c + 3 < DIRECT)
            def _():
                widen(jnp.minimum(c + 3, DIRECT - 1), 1)

            lower(c, 0)
            share(c, 0)

            @pl.when(c + 2 < DIRECT)
            def _():
                widen(jnp.minimum(c + 2, DIRECT - 1), 2)

            @pl.when(c + 1 == SECOND)
            def _():
                landed(SECOND, 1, True)

            @pl.when((c + 1 > SECOND) & (c + 1 < DIRECT))
            def _():
                landed(jnp.minimum(c + 1, DIRECT - 1), 2, False)

            @pl.when(c + 1 >= DIRECT)
            def _():
                arrived(rows.at[jnp.maximum(c + 1, DIRECT)], g_recv.at[jnp.maximum(c + 1, DIRECT), 2])

            unfold(c + 1)
            lower(c, 1)
            share(c, 1)
            return carry

        landed(FIRST, 1, True)
        unfold(FIRST)
        lax.fori_loop(0, CHUNKS - 1, batch, 0)
        lift()
        for h in range(2):
            lower(LAST, h)
            share(LAST, h)
        out[...] = jnp.zeros_like(out)
        sent(rows.at[0:DIRECT, 0, 0:3], g_send.at[0])
        sent(rows.at[2:DIRECT, 0:3], g_send.at[1])
        sent(rows.at[SECOND, 0:3], g_send.at[2])
        sent(turned, p_send.at[0])
        sent(parts, p_send.at[1])
        sent(passed.at[LAST], p_send.at[2])


def local(
    query, new_key, new_value, cache_key, cache_value, lengths, residual,
    norm_gain, router_weight, gate_weight, up_weight, down_weight, slot_rows, slot_count,
):
    vmem, smem, hbm = (
        pl.BlockSpec(memory_space=pltpu.VMEM),
        pl.BlockSpec(memory_space=pltpu.SMEM),
        pl.BlockSpec(memory_space=pl.ANY),
    )
    dma = pltpu.SemaphoreType.DMA
    return pl.pallas_call(
        kernel,
        out_shape=jax.ShapeDtypeStruct(query.shape, BF16),
        in_specs=[vmem, vmem, vmem, hbm, hbm, smem, vmem, vmem, vmem, hbm, hbm, hbm, smem, smem],
        out_specs=vmem,
        scratch_shapes=[
            pltpu.VMEM((ROW, CTX, KVH * HD), BF16),
            pltpu.VMEM((ROW, CTX, KVH * HD), BF16),
            pltpu.VMEM((ROW, D), F32),
            pltpu.VMEM((2 * ROW, FOLD), BF16),
            pltpu.VMEM((2, 2, 2 * ROW, QUARTER), BF16),
            pltpu.VMEM((CHUNKS, 2, 2 * ROW, QUARTER), BF16),
            pltpu.VMEM((CHUNKS, 4, 4, 2 * ROW, FOLD), BF16),
            pltpu.VMEM((CHUNKS, 2, 4, 4, 2 * ROW, QUARTER), BF16),
            pltpu.VMEM((CHUNKS, 2, 2, 4, 2 * ROW, QUARTER // 2), BF16),
            pltpu.VMEM((CHUNKS, 2, 2, 4, 2 * ROW, QUARTER), BF16),
            pltpu.VMEM((CHUNKS, 2, 4, 2 * ROW, QUARTER), BF16),
            pltpu.VMEM((CHUNKS, 2, 3, 2 * ROW, QUARTER), BF16),
            pltpu.VMEM((TILES, D, 2 * LANES), BF16),
            pltpu.VMEM((UNITS, D), BF16),
            pltpu.VMEM((BATCH, D), BF16),
            pltpu.VMEM((BATCH, LANES), F32),
            pltpu.VMEM((BATCH, UNITS), BF16),
            dma((2, 2)),
            dma((2,)),
            dma((1,)),
            dma((CHUNKS,)),
            dma((3,)),
            dma((CHUNKS, 3)),
            dma((3,)),
            dma((CHUNKS, 2)),
            dma((CHUNKS, 2)),
            dma((2,)),
            dma((CHUNKS, 3)),
            dma((1,)),
            dma((1,)),
        ],
        compiler_params=pltpu.CompilerParams(
            collective_id=0, has_side_effects=True, vmem_limit_bytes=56 * 2**20
        ),
        name="moe_block",
    )(
        query, new_key, new_value, cache_key, cache_value, lengths, residual,
        norm_gain.reshape(1, D), jnp.transpose(router_weight),
        gate_weight, up_weight, down_weight, slot_rows, slot_count,
    )


def solution(mesh):
    return jax.shard_map(
        local,
        mesh=mesh,
        in_specs=(
            P("side", "dev", None, None),
            P("side", "dev", None, None),
            P("side", "dev", None, None),
            P("side", "dev", None, None, None),
            P("side", "dev", None, None, None),
            P("side", "dev", None),
            P("side", "dev", None, None),
            P(),
            P(),
            P("side", None, "dev"),
            P("side", None, "dev"),
            P("side", "dev", None),
            P("side", "dev", None, None),
            P("side", "dev", None),
        ),
        out_specs=P("side", "dev", None, None),
        check_vma=False,
    )
```

```python
import functools
import math

import jax
import jax.numpy as jnp
from jax import lax
from jax.experimental import pallas as pl
from jax.experimental.pallas import tpu as pltpu
from jax.sharding import PartitionSpec as P

MESH = pl.DeviceIdType.MESH
F32 = jnp.float32
BF16 = jnp.bfloat16

HD = 128
KVH = 8
GROUP = 4
EXP = 4
ROW = 8
CTX = 128
D = 4096
HALF = D // 2
QUARTER = D // 4
LANES = 128
FOLD = HALF + LANES
UNITS = 896
TILES = UNITS // LANES
CHUNKS = 6
SPANS = ((0, QUARTER), (QUARTER, FOLD))
BATCH = 16 * ROW
FIRST, SECOND, LAST, LIFTED = 0, 1, 4, 5
PASSED = 0
DIRECT = 5
NEG = -1e30


def cols(start, stop):
    return pl.ds(start, stop - start)


def attention(q, nk, nv, ck, cv, lengths, res, gain, router, slot_rows, slot_count, kbuf, vbuf, stream, pay, sems):
    pieces = 2
    wide = KVH * HD // pieces

    def load(source, target, which, piece):
        span = pl.ds(piece * wide, wide)
        return pltpu.make_async_copy(source.at[:, :, span], target.at[:, :, span], sems.at[which, piece])

    for piece in range(pieces):
        load(ck, kbuf, 0, piece).start()
        load(cv, vbuf, 1, piece).start()
    scale = 1.0 / math.sqrt(HD)
    sub = lax.broadcasted_iota(jnp.int32, (ROW, LANES), 0)
    lane = lax.broadcasted_iota(jnp.int32, (ROW, LANES), 1)
    length = jnp.zeros((ROW, LANES), jnp.int32)
    for r in range(ROW):
        length = jnp.where(sub == r, lengths[0, 0, r], length)
    seen = jnp.concatenate([lane < length] * GROUP, axis=0)
    row = jnp.concatenate([sub] * GROUP, axis=0)
    spans = [slice(k * HD, (k + 1) * HD) for k in range(KVH)]
    scores, own, new_values = [], [], []
    for k, span in enumerate(spans):
        if k % (KVH // pieces) == 0:
            load(ck, kbuf, 0, k // (KVH // pieces)).wait()
        heads = [slice((k * GROUP + g) * HD, (k * GROUP + g + 1) * HD) for g in range(GROUP)]
        query = jnp.concatenate([q[0, 0, :, h].astype(F32) for h in heads], axis=0)
        new_key = jnp.concatenate([nk[0, 0, :, span].astype(F32)] * GROUP, axis=0)
        new_values.append(jnp.concatenate([nv[0, 0, :, span].astype(F32)] * GROUP, axis=0))
        keys = kbuf[:, :, span].reshape(ROW * CTX, HD)
        every = lax.dot_general(query.astype(BF16), keys, (((1,), (1,)), ((), ())), preferred_element_type=F32)
        kept = every[:, 0:CTX]
        for r in range(1, ROW):
            kept = jnp.where(row == r, every[:, r * CTX : (r + 1) * CTX], kept)
        scores.append(jnp.where(seen, kept * scale, NEG))
        own.append(jnp.sum(query * new_key, axis=1, keepdims=True) * scale)
    weights, own_weights = [], []
    for k in range(KVH):
        top = jnp.maximum(jnp.max(scores[k], axis=1, keepdims=True), own[k])
        probs = jnp.exp(scores[k] - top)
        own_prob = jnp.exp(own[k] - top)
        inverse = 1.0 / (jnp.sum(probs, axis=1, keepdims=True) + own_prob)
        weights.append(probs * inverse)
        own_weights.append((own_prob * inverse).astype(BF16).astype(F32))
    total = jnp.zeros((ROW, LANES), F32)
    for k, span in enumerate(spans):
        if k % (KVH // pieces) == 0:
            load(cv, vbuf, 1, k // (KVH // pieces)).wait()
        values = vbuf[:, :, span].reshape(ROW * CTX, HD)
        spaced = jnp.concatenate([jnp.where(row == r, weights[k], 0.0).astype(BF16) for r in range(ROW)], axis=1)
        context = jnp.dot(spaced, values, preferred_element_type=F32) + own_weights[k] * new_values[k]
        for g in range(GROUP):
            h = slice((k * GROUP + g) * HD, (k * GROUP + g + 1) * HD)
            part = res[0, 0, :, h].astype(F32) + context[g * ROW : (g + 1) * ROW]
            stream[:, h] = part
            total = total + part * part
    total = jnp.sum(total, axis=1, keepdims=True)
    rows = stream[...]
    normed = (rows * lax.rsqrt(total / D + 1e-05) * gain[...]).astype(BF16)
    logits = lax.dot_general(normed, router[...], (((1,), (1,)), ((), ())), preferred_element_type=F32)
    raised = []
    for e in range(EXP):
        chosen = jnp.zeros((ROW, 1), F32)
        for c in range(slot_rows.shape[3]):
            hit = (sub[:, 0:1] == slot_rows[0, 0, e, c]) & (c < slot_count[0, 0, e])
            chosen = chosen + jnp.where(hit, 1.0, 0.0)
        raised.append(chosen * jnp.exp(logits[:, e : e + 1]))
    inverse = raised[0] + raised[1] + raised[2] + raised[3]
    table = jnp.zeros((ROW, LANES), F32)
    for e in range(EXP):
        weight = raised[e] / inverse
        high = weight.astype(BF16).astype(F32)
        table = table + jnp.where(lane == e, high, 0.0) + jnp.where(lane == EXP + e, weight - high, 0.0)
    normed = normed.astype(F32)
    upper = [normed[:, 0:QUARTER], normed[:, HALF : HALF + QUARTER], table]
    lower = [normed[:, QUARTER:HALF], normed[:, HALF + QUARTER : D], jnp.zeros((ROW, LANES), F32)]
    pay[...] = jnp.concatenate([jnp.concatenate(upper, axis=1), jnp.concatenate(lower, axis=1)], axis=0).astype(BF16)


def kernel(
    q, nk, nv, ck, cv, lengths, res, gain, router, gate, up, down, slot_rows, slot_count,
    out,
    kbuf, vbuf, stream, pay, back, done,
    rows, parts, turned, passed, merged, crossed, wide, wdown, block, weight, hidden,
    kv_sems, w_sems, pay_send, pay_recv, g_send, g_recv, p_send, p_recv, own_recv, r_send, r_recv, b_send, b_recv,
):
    side, me = lax.axis_index("side"), lax.axis_index("dev")
    z, x, y = me // 16, lax.rem(me // 4, 4), lax.rem(me, 4)
    xs = [x] + [lax.rem(x + k, 4) for k in (1, 2, 3)]
    ys = [y] + [lax.rem(y + k, 4) for k in (1, 2, 3)]

    def at(z, x, y):
        return z * 16 + x * 4 + y

    near, far = at(1 - z, x, y), me
    in_line = [at(z, xs[k], y) for k in (1, 2, 3)] + [at(z, x, ys[k]) for k in (1, 2, 3)]
    barrier = pltpu.get_barrier_semaphore()

    def greet(side, dev):
        pl.semaphore_signal(barrier, inc=1, device_id={"side": side, "dev": dev}, device_id_type=MESH)

    def remote(src, dst, send, recv, side, dev):
        return pltpu.make_async_remote_copy(
            src_ref=src, dst_ref=dst, send_sem=send, recv_sem=recv,
            device_id={"side": side, "dev": dev}, device_id_type=MESH,
        )

    is_far_pod, is_hub, is_expert = side < 2, side == 2, side == 3

    @pl.when(is_far_pod)
    def _():
        for s in (2, 3):
            greet(s, near)
            greet(s, far)
        for dev in in_line:
            greet(side, dev)

    @pl.when(jnp.logical_not(is_far_pod))
    def _():
        for s in (2, 3):
            for dev in in_line:
                greet(s, dev)
        greet(5 - side, me)
        greet(5 - side, near)
        for s in (0, 1):
            greet(s, near)
            greet(s, far)

    @pl.when(is_hub)
    def _():
        greet(2, near)

    def load_weights():
        for n in range(TILES):
            span = pl.ds(n * LANES, LANES)
            pltpu.make_async_copy(gate.at[0, :, span], wide.at[n, :, pl.ds(0, LANES)], w_sems.at[0]).start()
            pltpu.make_async_copy(up.at[0, :, span], wide.at[n, :, pl.ds(LANES, LANES)], w_sems.at[0]).start()
        pltpu.make_async_copy(down.at[0], wdown, w_sems.at[1]).start()

    @pl.when(is_expert)
    def _():
        load_weights()

    @pl.when(jnp.logical_not(is_expert))
    def _():
        attention(
            q, nk, nv, ck.at[0, 0], cv.at[0, 0], lengths, res, gain, router, slot_rows, slot_count,
            kbuf, vbuf, stream, pay, kv_sems,
        )

    pl.semaphore_wait(barrier, jnp.where(is_hub, 19, jnp.where(is_expert, 18, 10)))

    def finish():
        for h in range(2):
            mix = back[0, h].astype(F32) + back[1, h].astype(F32)
            for k in range(2):
                span = slice((2 * h + k) * QUARTER, (2 * h + k + 1) * QUARTER)
                part = mix[k * ROW : (k + 1) * ROW].astype(BF16).astype(F32)
                out[0, 0, :, span] = (stream[:, span] + part).astype(BF16)

    def arrived(ref, sem):
        remote(ref, ref, pay_send.at[0], sem, side, me).wait_recv()

    def sent(ref, sem):
        remote(ref, ref, sem, pay_recv.at[0], side, me).wait_send()

    def give_rows(c, dev):
        remote(pay, rows.at[c, y, x], pay_send.at[0], pay_recv.at[c], 3, dev).start()

    here = (ys, xs)
    line_devs = ([at(z, x, ys[k]) for k in range(4)], [at(z, xs[k], y) for k in range(4)])

    def band(ref, h, j, span=slice(None)):
        return ref.at[j, :, :, span] if h == 0 else ref.at[:, j, :, span]

    def spread(c, phase, straight):
        for h in range(2):
            begin, stop = SPANS[h]
            whole = cols(begin, stop)
            halves = cols(begin, begin + QUARTER // 2), cols(begin + QUARTER // 2, stop)

            def send(ref, which, dev):
                remote(ref, ref, g_send.at[which], g_recv.at[c, phase], side, dev).start()

            if phase == 0:
                for k in (1, 2, 3):
                    send(rows.at[c, y, x, :, whole], 0, line_devs[1 - h][k])
            elif phase == 1:
                for k in (1, 3, 2) if straight else (1, 3):
                    send(band(rows.at[c], h, here[h][0], whole), 2 if straight else 1, line_devs[h][k])
            else:
                send(band(rows.at[c], h, here[h][3], halves[0]), 1, line_devs[h][1])
                send(band(rows.at[c], h, here[h][1], halves[1]), 1, line_devs[h][3])

    def landed(c, phase, straight):
        ref = rows.at[c, 0, 0:3] if phase == 0 else rows.at[c, 0 : 3 if straight else 3 - phase]
        arrived(ref, g_recv.at[c, phase])

    @pl.when(is_far_pod)
    def _():
        @pl.when(side == 1)
        def _():
            give_rows(SECOND, near)
            give_rows(3, far)
            sent(rows.at[0, 0, 0:2], pay_send.at[0])

        @pl.when(side == 0)
        def _():
            rows[LIFTED, y, x] = pay[...]
            spread(LIFTED, 0, True)
            give_rows(2, far)
            landed(LIFTED, 0, True)
            spread(LIFTED, 1, True)

            def push(k):
                for h in range(2):
                    ref = band(rows.at[LIFTED], h, here[h][k], cols(*SPANS[h]))
                    remote(ref, ref, p_send.at[0], g_recv.at[LIFTED, 2], 3, near).start()

            push(0)
            landed(LIFTED, 1, True)
            for k in (1, 3, 2):
                push(k)
            sent(rows.at[0, 0, 0:1], pay_send.at[0])
            sent(rows.at[LIFTED, 0, 0:3], g_send.at[0])
            sent(rows.at[LIFTED, 0:3], g_send.at[2])
            sent(rows.at[LIFTED], p_send.at[0])

        arrived(back, b_recv.at[0])
        finish()

    @pl.when(is_hub)
    def _():
        give_rows(FIRST, near)
        give_rows(LAST, me)

        def cell(c, h, j, i):
            return parts.at[c, h, j, i] if h == 0 else parts.at[c, h, i, j]

        def first(c, h):
            arrived(parts.at[c, h], own_recv.at[c, h])
            arrived(turned.at[c, h], p_recv.at[c, h])
            if c >= PASSED:
                return
            for k, step in enumerate((1, 3)):
                span = slice(k * QUARTER // 2, (k + 1) * QUARTER // 2)
                for i in range(4):
                    ref = cell(c, h, here[h][step], i).at[:, span]
                    ref[...] = (ref[...].astype(F32) + turned[c, h, k, i].astype(F32)).astype(BF16)
                src = band(parts.at[c, h], h, here[h][step])
                remote(src, passed.at[c, h, k], r_send.at[0], r_recv.at[c, h], 2, line_devs[h][step]).start()

        def middle(c, h):
            arrived(passed.at[c, h], r_recv.at[c, h])
            for i in range(4):
                total = cell(c, h, here[h][0], i)[...].astype(F32) + passed[c, h, 0, i].astype(F32)
                total = total + passed[c, h, 1, i].astype(F32)
                if c >= PASSED:
                    halves = [turned[c, h, k, i].astype(F32) for k in range(2)]
                    total = total + jnp.concatenate(halves, axis=1)
                merged[c, h, i] = total.astype(BF16)
            for k in range(1, 4):
                src, dst = merged.at[c, h, here[1 - h][k]], crossed.at[c, h, k - 1]
                remote(src, dst, r_send.at[1], r_recv.at[c, 2], 2, line_devs[1 - h][k]).start()

        def second(c):
            target = back.at[0] if c == LAST else done.at[c]
            arrived(crossed.at[c], r_recv.at[c, 2])
            for h in range(2):
                total = merged[c, h, here[1 - h][0]].astype(F32)
                for k in range(3):
                    total = total + crossed[c, h, k].astype(F32)
                target[h] = total.astype(BF16)
            if c != LAST:
                owners = (2, near, 1), (1, near, 0), (0, far, 1), (1, far, 1), None, (0, near, 0)
                owner, dev, k = owners[c]
                remote(done.at[c], back.at[k], b_send.at[0], b_recv.at[0], owner, dev).start()

        def both(step, c):
            for h in range(2):
                step(c, h)

        order = (0, 1, 2, 3, LIFTED, LAST)
        for i, c in enumerate(order):
            if c < PASSED:
                both(first, c)
                if i > 0:
                    both(middle, order[i - 1])
            else:
                if order[i - 1] < PASSED and i > 0:
                    both(middle, order[i - 1])
                both(first, c)
                both(middle, c)
            if i > 1:
                second(order[i - 2])
        second(LIFTED)
        second(LAST)
        arrived(back.at[1], b_recv.at[0])
        finish()
        sent(rows.at[0, 0, 0:2], pay_send.at[0])
        sent(crossed, r_send.at[1])
        sent(done.at[1:CHUNKS], b_send.at[0])

    @pl.when(is_expert)
    def _():
        expert = me // 8

        def is_last(c):
            return isinstance(c, int) and c == LAST

        def widen(c, phase, straight=False):
            landed(c, phase - 1, straight)
            spread(c, phase, straight)

        def share(c, h):
            ref = parts.at[c, h]

            def send(straight):
                for k, step in enumerate((1, 3)):
                    src = band(ref, h, here[h][2], pl.ds(k * QUARTER // 2, QUARTER // 2))
                    dev = line_devs[h][2 if straight else step]
                    remote(src, turned.at[c, h, k], p_send.at[0], p_recv.at[c, h], 2, dev).start()
                    if straight:
                        src = band(ref, h, here[h][step])
                        remote(src, passed.at[c, h, 1 - k], p_send.at[2], r_recv.at[c, h], 2, line_devs[h][step]).start()

            if is_last(c):
                send(True)
            else:
                send(True)
            remote(ref, ref, p_send.at[1], own_recv.at[c, h], 2, me).start()

        for c in range(DIRECT):
            arrived(rows.at[c, y, x], pay_recv.at[c])
            spread(c, 0, False)
        widen(FIRST, 1, True)
        sent(rows.at[FIRST, 0:3], g_send.at[2])
        widen(SECOND, 1, True)
        widen(2, 1)
        pltpu.make_async_copy(wide, wide, w_sems.at[0]).wait()
        pltpu.make_async_copy(wdown, wdown, w_sems.at[1]).wait()
        lane = lax.broadcasted_iota(jnp.int32, (ROW, LANES), 1)
        mine = (lane == expert) | (lane == expert + EXP)

        def unfold(c):
            for i in range(8):
                pair = [rows[c, i // 2, 2 * (i % 2) + k].astype(F32) for k in range(2)]
                to = slice(i * 2 * ROW, (i + 1) * 2 * ROW)
                for k in range(4):
                    row, begin = (k % 2) * ROW, (k // 2) * QUARTER
                    piece = [p[row : row + ROW, begin : begin + QUARTER] for p in pair]
                    block[to, k * QUARTER : (k + 1) * QUARTER] = jnp.concatenate(piece, axis=0).astype(BF16)
                table = [jnp.where(mine, p[0:ROW, HALF:FOLD], 0.0) for p in pair]
                table = [jnp.broadcast_to(jnp.sum(t, axis=1, keepdims=True), (ROW, LANES)) for t in table]
                weight[to, :] = jnp.concatenate(table, axis=0)

        def lift():
            for n in range(TILES):
                both = jnp.dot(block[...], wide[n], preferred_element_type=F32)
                g, u = both[:, 0:LANES], both[:, LANES:]
                hidden[:, n * LANES : (n + 1) * LANES] = (g * u / (1.0 + jnp.exp(-g)) * weight[...]).astype(BF16)

        def lower(c, h):
            made = jnp.dot(hidden[...], wdown[:, h * HALF : (h + 1) * HALF], preferred_element_type=F32)
            made = made.reshape(16, ROW, HALF)
            made = jnp.concatenate([made[:, :, 0:QUARTER], made[:, :, QUARTER:HALF]], axis=1)
            parts[c, h] = made.astype(BF16).reshape(4, 4, 2 * ROW, QUARTER)

        def batch(i, carry):
            c = jnp.where(i < LAST, i, LIFTED)
            after = jnp.where(i < LAST - 1, i + 1, jnp.where(i < LAST, LIFTED, LAST))

            @pl.when(i + 3 < DIRECT)
            def _():
                widen(jnp.minimum(i + 3, DIRECT - 1), 1)

            lift()

            @pl.when(i + 2 < DIRECT)
            def _():
                widen(jnp.minimum(i + 2, DIRECT - 1), 2)

            lower(c, 0)
            share(c, 0)

            @pl.when(i + 1 == SECOND)
            def _():
                landed(SECOND, 1, True)

            @pl.when((i + 1 > SECOND) & (i != LAST - 1))
            def _():
                landed(jnp.minimum(after, LAST), 2, False)

            @pl.when(i == LAST - 1)
            def _():
                arrived(rows.at[LIFTED], g_recv.at[LIFTED, 2])

            unfold(after)
            lower(c, 1)
            share(c, 1)
            return carry

        landed(FIRST, 1, True)
        unfold(FIRST)
        lax.fori_loop(0, CHUNKS - 1, batch, 0)
        lift()
        for h in range(2):
            lower(LAST, h)
            share(LAST, h)
        out[...] = jnp.zeros_like(out)
        sent(rows.at[0:DIRECT, 0, 0:3], g_send.at[0])
        sent(rows.at[2:DIRECT, 0:3], g_send.at[1])
        sent(rows.at[SECOND, 0:3], g_send.at[2])
        sent(turned, p_send.at[0])
        sent(parts, p_send.at[1])
        sent(passed.at[PASSED:CHUNKS], p_send.at[2])


def local(
    query, new_key, new_value, cache_key, cache_value, lengths, residual,
    norm_gain, router_weight, gate_weight, up_weight, down_weight, slot_rows, slot_count,
):
    vmem, smem, hbm = (
        pl.BlockSpec(memory_space=pltpu.VMEM),
        pl.BlockSpec(memory_space=pltpu.SMEM),
        pl.BlockSpec(memory_space=pl.ANY),
    )
    dma = pltpu.SemaphoreType.DMA
    return pl.pallas_call(
        kernel,
        out_shape=jax.ShapeDtypeStruct(query.shape, BF16),
        in_specs=[vmem, vmem, vmem, hbm, hbm, smem, vmem, vmem, vmem, hbm, hbm, hbm, smem, smem],
        out_specs=vmem,
        scratch_shapes=[
            pltpu.VMEM((ROW, CTX, KVH * HD), BF16),
            pltpu.VMEM((ROW, CTX, KVH * HD), BF16),
            pltpu.VMEM((ROW, D), F32),
            pltpu.VMEM((2 * ROW, FOLD), BF16),
            pltpu.VMEM((2, 2, 2 * ROW, QUARTER), BF16),
            pltpu.VMEM((CHUNKS, 2, 2 * ROW, QUARTER), BF16),
            pltpu.VMEM((CHUNKS, 4, 4, 2 * ROW, FOLD), BF16),
            pltpu.VMEM((CHUNKS, 2, 4, 4, 2 * ROW, QUARTER), BF16),
            pltpu.VMEM((CHUNKS, 2, 2, 4, 2 * ROW, QUARTER // 2), BF16),
            pltpu.VMEM((CHUNKS, 2, 2, 4, 2 * ROW, QUARTER), BF16),
            pltpu.VMEM((CHUNKS, 2, 4, 2 * ROW, QUARTER), BF16),
            pltpu.VMEM((CHUNKS, 2, 3, 2 * ROW, QUARTER), BF16),
            pltpu.VMEM((TILES, D, 2 * LANES), BF16),
            pltpu.VMEM((UNITS, D), BF16),
            pltpu.VMEM((BATCH, D), BF16),
            pltpu.VMEM((BATCH, LANES), F32),
            pltpu.VMEM((BATCH, UNITS), BF16),
            dma((2, 2)),
            dma((2,)),
            dma((1,)),
            dma((CHUNKS,)),
            dma((3,)),
            dma((CHUNKS, 3)),
            dma((3,)),
            dma((CHUNKS, 2)),
            dma((CHUNKS, 2)),
            dma((2,)),
            dma((CHUNKS, 3)),
            dma((1,)),
            dma((1,)),
        ],
        compiler_params=pltpu.CompilerParams(
            collective_id=0, has_side_effects=True, vmem_limit_bytes=56 * 2**20
        ),
        name="moe_block",
    )(
        query, new_key, new_value, cache_key, cache_value, lengths, residual,
        norm_gain.reshape(1, D), jnp.transpose(router_weight),
        gate_weight, up_weight, down_weight, slot_rows, slot_count,
    )


def solution(mesh):
    return jax.shard_map(
        local,
        mesh=mesh,
        in_specs=(
            P("side", "dev", None, None),
            P("side", "dev", None, None),
            P("side", "dev", None, None),
            P("side", "dev", None, None, None),
            P("side", "dev", None, None, None),
            P("side", "dev", None),
            P("side", "dev", None, None),
            P(),
            P(),
            P("side", None, "dev"),
            P("side", None, "dev"),
            P("side", "dev", None),
            P("side", "dev", None, None),
            P("side", "dev", None),
        ),
        out_specs=P("side", "dev", None, None),
        check_vma=False,
    )
```

```python
import functools
import math

import jax
import jax.numpy as jnp
from jax import lax
from jax.experimental import pallas as pl
from jax.experimental.pallas import tpu as pltpu
from jax.sharding import PartitionSpec as P

MESH = pl.DeviceIdType.MESH
F32 = jnp.float32
BF16 = jnp.bfloat16

HD = 128
KVH = 8
GROUP = 4
EXP = 4
ROW = 8
CTX = 128
D = 4096
HALF = D // 2
QUARTER = D // 4
LANES = 128
FOLD = HALF + LANES
UNITS = 896
TILES = UNITS // LANES
CHUNKS = 6
SPANS = ((0, QUARTER), (QUARTER, FOLD))
BATCH = 16 * ROW
FIRST, SECOND, LAST, LIFTED = 0, 1, 4, 5
PASSED = 0
DIRECT = 5
NEG = -1e30


def cols(start, stop):
    return pl.ds(start, stop - start)


def attention(q, nk, nv, ck, cv, lengths, res, gain, router, slot_rows, slot_count, kbuf, vbuf, stream, pay, sems):
    pieces = 2
    wide = KVH * HD // pieces

    def load(source, target, which, piece):
        span = pl.ds(piece * wide, wide)
        return pltpu.make_async_copy(source.at[:, :, span], target.at[:, :, span], sems.at[which, piece])

    for piece in range(pieces):
        load(ck, kbuf, 0, piece).start()
        load(cv, vbuf, 1, piece).start()
    scale = 1.0 / math.sqrt(HD)
    sub = lax.broadcasted_iota(jnp.int32, (ROW, LANES), 0)
    lane = lax.broadcasted_iota(jnp.int32, (ROW, LANES), 1)
    length = jnp.zeros((ROW, LANES), jnp.int32)
    for r in range(ROW):
        length = jnp.where(sub == r, lengths[0, 0, r], length)
    seen = jnp.concatenate([lane < length] * GROUP, axis=0)
    row = jnp.concatenate([sub] * GROUP, axis=0)
    spans = [slice(k * HD, (k + 1) * HD) for k in range(KVH)]
    scores, own, new_values = [], [], []
    for k, span in enumerate(spans):
        if k % (KVH // pieces) == 0:
            load(ck, kbuf, 0, k // (KVH // pieces)).wait()
        heads = [slice((k * GROUP + g) * HD, (k * GROUP + g + 1) * HD) for g in range(GROUP)]
        query = jnp.concatenate([q[0, 0, :, h].astype(F32) for h in heads], axis=0)
        new_key = jnp.concatenate([nk[0, 0, :, span].astype(F32)] * GROUP, axis=0)
        new_values.append(jnp.concatenate([nv[0, 0, :, span].astype(F32)] * GROUP, axis=0))
        keys = kbuf[:, :, span].reshape(ROW * CTX, HD)
        every = lax.dot_general(query.astype(BF16), keys, (((1,), (1,)), ((), ())), preferred_element_type=F32)
        kept = every[:, 0:CTX]
        for r in range(1, ROW):
            kept = jnp.where(row == r, every[:, r * CTX : (r + 1) * CTX], kept)
        scores.append(jnp.where(seen, kept * scale, NEG))
        own.append(jnp.sum(query * new_key, axis=1, keepdims=True) * scale)
    weights, own_weights = [], []
    for k in range(KVH):
        top = jnp.maximum(jnp.max(scores[k], axis=1, keepdims=True), own[k])
        probs = jnp.exp(scores[k] - top)
        own_prob = jnp.exp(own[k] - top)
        inverse = 1.0 / (jnp.sum(probs, axis=1, keepdims=True) + own_prob)
        weights.append(probs * inverse)
        own_weights.append((own_prob * inverse).astype(BF16).astype(F32))
    total = jnp.zeros((ROW, LANES), F32)
    for k, span in enumerate(spans):
        if k % (KVH // pieces) == 0:
            load(cv, vbuf, 1, k // (KVH // pieces)).wait()
        values = vbuf[:, :, span].reshape(ROW * CTX, HD)
        spaced = jnp.concatenate([jnp.where(row == r, weights[k], 0.0).astype(BF16) for r in range(ROW)], axis=1)
        context = jnp.dot(spaced, values, preferred_element_type=F32) + own_weights[k] * new_values[k]
        for g in range(GROUP):
            h = slice((k * GROUP + g) * HD, (k * GROUP + g + 1) * HD)
            part = res[0, 0, :, h].astype(F32) + context[g * ROW : (g + 1) * ROW]
            stream[:, h] = part
            total = total + part * part
    total = jnp.sum(total, axis=1, keepdims=True)
    rows = stream[...]
    normed = (rows * lax.rsqrt(total / D + 1e-05) * gain[...]).astype(BF16)
    logits = lax.dot_general(normed, router[...], (((1,), (1,)), ((), ())), preferred_element_type=F32)
    raised = []
    for e in range(EXP):
        chosen = jnp.zeros((ROW, 1), F32)
        for c in range(slot_rows.shape[3]):
            hit = (sub[:, 0:1] == slot_rows[0, 0, e, c]) & (c < slot_count[0, 0, e])
            chosen = chosen + jnp.where(hit, 1.0, 0.0)
        raised.append(chosen * jnp.exp(logits[:, e : e + 1]))
    inverse = raised[0] + raised[1] + raised[2] + raised[3]
    table = jnp.zeros((ROW, LANES), F32)
    for e in range(EXP):
        weight = raised[e] / inverse
        high = weight.astype(BF16).astype(F32)
        table = table + jnp.where(lane == e, high, 0.0) + jnp.where(lane == EXP + e, weight - high, 0.0)
    normed = normed.astype(F32)
    upper = [normed[:, 0:QUARTER], normed[:, HALF : HALF + QUARTER], table]
    lower = [normed[:, QUARTER:HALF], normed[:, HALF + QUARTER : D], jnp.zeros((ROW, LANES), F32)]
    pay[...] = jnp.concatenate([jnp.concatenate(upper, axis=1), jnp.concatenate(lower, axis=1)], axis=0).astype(BF16)


def kernel(
    q, nk, nv, ck, cv, lengths, res, gain, router, gate, up, down, slot_rows, slot_count,
    out,
    kbuf, vbuf, stream, pay, back, done,
    rows, parts, turned, passed, merged, crossed, wide, wdown, block, weight, hidden,
    kv_sems, w_sems, pay_send, pay_recv, g_send, g_recv, p_send, p_recv, own_recv, r_send, r_recv, b_send, b_recv,
):
    side, me = lax.axis_index("side"), lax.axis_index("dev")
    z, x, y = me // 16, lax.rem(me // 4, 4), lax.rem(me, 4)
    xs = [x] + [lax.rem(x + k, 4) for k in (1, 2, 3)]
    ys = [y] + [lax.rem(y + k, 4) for k in (1, 2, 3)]

    def at(z, x, y):
        return z * 16 + x * 4 + y

    near, far = at(1 - z, x, y), me
    in_line = [at(z, xs[k], y) for k in (1, 2, 3)] + [at(z, x, ys[k]) for k in (1, 2, 3)]
    barrier = pltpu.get_barrier_semaphore()

    def greet(side, dev):
        pl.semaphore_signal(barrier, inc=1, device_id={"side": side, "dev": dev}, device_id_type=MESH)

    def remote(src, dst, send, recv, side, dev):
        return pltpu.make_async_remote_copy(
            src_ref=src, dst_ref=dst, send_sem=send, recv_sem=recv,
            device_id={"side": side, "dev": dev}, device_id_type=MESH,
        )

    is_far_pod, is_hub, is_expert = side < 2, side == 2, side == 3

    @pl.when(is_far_pod)
    def _():
        for s in (2, 3):
            greet(s, near)
            greet(s, far)
        for dev in in_line:
            greet(side, dev)

    @pl.when(jnp.logical_not(is_far_pod))
    def _():
        for s in (2, 3):
            for dev in in_line:
                greet(s, dev)
        greet(5 - side, me)
        greet(5 - side, near)
        for s in (0, 1):
            greet(s, near)
            greet(s, far)

    @pl.when(is_hub)
    def _():
        greet(2, near)

    def load_weights():
        for n in range(TILES):
            span = pl.ds(n * LANES, LANES)
            pltpu.make_async_copy(gate.at[0, :, span], wide.at[n, :, pl.ds(0, LANES)], w_sems.at[0]).start()
            pltpu.make_async_copy(up.at[0, :, span], wide.at[n, :, pl.ds(LANES, LANES)], w_sems.at[0]).start()
        pltpu.make_async_copy(down.at[0], wdown, w_sems.at[1]).start()

    @pl.when(is_expert)
    def _():
        load_weights()

    @pl.when(jnp.logical_not(is_expert))
    def _():
        attention(
            q, nk, nv, ck.at[0, 0], cv.at[0, 0], lengths, res, gain, router, slot_rows, slot_count,
            kbuf, vbuf, stream, pay, kv_sems,
        )

    pl.semaphore_wait(barrier, jnp.where(is_hub, 19, jnp.where(is_expert, 18, 10)))

    def finish():
        for h in range(2):
            mix = back[0, h].astype(F32) + back[1, h].astype(F32)
            for k in range(2):
                span = slice((2 * h + k) * QUARTER, (2 * h + k + 1) * QUARTER)
                part = mix[k * ROW : (k + 1) * ROW].astype(BF16).astype(F32)
                out[0, 0, :, span] = (stream[:, span] + part).astype(BF16)

    def arrived(ref, sem):
        remote(ref, ref, pay_send.at[0], sem, side, me).wait_recv()

    def sent(ref, sem):
        remote(ref, ref, sem, pay_recv.at[0], side, me).wait_send()

    def give_rows(c, dev):
        remote(pay, rows.at[c, y, x], pay_send.at[0], pay_recv.at[c], 3, dev).start()

    here = (ys, xs)
    line_devs = ([at(z, x, ys[k]) for k in range(4)], [at(z, xs[k], y) for k in range(4)])

    def band(ref, h, j, span=slice(None)):
        return ref.at[j, :, :, span] if h == 0 else ref.at[:, j, :, span]

    def spread(c, phase, straight):
        for h in range(2):
            begin, stop = SPANS[h]
            whole = cols(begin, stop)
            halves = cols(begin, begin + QUARTER // 2), cols(begin + QUARTER // 2, stop)

            def send(ref, which, dev):
                remote(ref, ref, g_send.at[which], g_recv.at[c, phase], side, dev).start()

            if phase == 0:
                for k in (1, 2, 3):
                    send(rows.at[c, y, x, :, whole], 0, line_devs[1 - h][k])
            elif phase == 1:
                for k in (1, 3, 2) if straight else (1, 3):
                    send(band(rows.at[c], h, here[h][0], whole), 2 if straight else 1, line_devs[h][k])
            else:
                send(band(rows.at[c], h, here[h][3], halves[0]), 1, line_devs[h][1])
                send(band(rows.at[c], h, here[h][1], halves[1]), 1, line_devs[h][3])

    def landed(c, phase, straight):
        ref = rows.at[c, 0, 0:3] if phase == 0 else rows.at[c, 0 : 3 if straight else 3 - phase]
        arrived(ref, g_recv.at[c, phase])

    @pl.when(is_far_pod)
    def _():
        @pl.when(side == 1)
        def _():
            give_rows(SECOND, near)
            give_rows(3, far)
            sent(rows.at[0, 0, 0:2], pay_send.at[0])

        @pl.when(side == 0)
        def _():
            rows[LIFTED, y, x] = pay[...]
            spread(LIFTED, 0, True)
            give_rows(2, far)
            landed(LIFTED, 0, True)
            spread(LIFTED, 1, True)

            def push(k):
                for h in range(2):
                    ref = band(rows.at[LIFTED], h, here[h][k], cols(*SPANS[h]))
                    remote(ref, ref, p_send.at[0], g_recv.at[LIFTED, 2], 3, near).start()

            push(0)
            landed(LIFTED, 1, True)
            for k in (1, 3, 2):
                push(k)
            sent(rows.at[0, 0, 0:1], pay_send.at[0])
            sent(rows.at[LIFTED, 0, 0:3], g_send.at[0])
            sent(rows.at[LIFTED, 0:3], g_send.at[2])
            sent(rows.at[LIFTED], p_send.at[0])

        arrived(back, b_recv.at[0])
        finish()

    @pl.when(is_hub)
    def _():
        give_rows(FIRST, near)
        give_rows(LAST, me)

        def cell(c, h, j, i):
            return parts.at[c, h, j, i] if h == 0 else parts.at[c, h, i, j]

        def first(c, h):
            arrived(band(parts.at[c, h], h, here[h][0]), own_recv.at[c, h])
            arrived(turned.at[c, h], p_recv.at[c, h])
            if c >= PASSED:
                return
            for k, step in enumerate((1, 3)):
                span = slice(k * QUARTER // 2, (k + 1) * QUARTER // 2)
                for i in range(4):
                    ref = cell(c, h, here[h][step], i).at[:, span]
                    ref[...] = (ref[...].astype(F32) + turned[c, h, k, i].astype(F32)).astype(BF16)
                src = band(parts.at[c, h], h, here[h][step])
                remote(src, passed.at[c, h, k], r_send.at[0], r_recv.at[c, h], 2, line_devs[h][step]).start()

        def middle(c, h):
            arrived(passed.at[c, h], r_recv.at[c, h])
            for i in range(4):
                total = cell(c, h, here[h][0], i)[...].astype(F32) + passed[c, h, 0, i].astype(F32)
                total = total + passed[c, h, 1, i].astype(F32)
                if c >= PASSED:
                    halves = [turned[c, h, k, i].astype(F32) for k in range(2)]
                    total = total + jnp.concatenate(halves, axis=1)
                merged[c, h, i] = total.astype(BF16)
            for k in range(1, 4):
                src, dst = merged.at[c, h, here[1 - h][k]], crossed.at[c, h, k - 1]
                remote(src, dst, r_send.at[1], r_recv.at[c, 2], 2, line_devs[1 - h][k]).start()

        def second(c):
            target = back.at[0] if c == LAST else done.at[c]
            arrived(crossed.at[c], r_recv.at[c, 2])
            for h in range(2):
                total = merged[c, h, here[1 - h][0]].astype(F32)
                for k in range(3):
                    total = total + crossed[c, h, k].astype(F32)
                target[h] = total.astype(BF16)
            if c != LAST:
                owners = (2, near, 1), (1, near, 0), (0, far, 1), (1, far, 1), None, (0, near, 0)
                owner, dev, k = owners[c]
                remote(done.at[c], back.at[k], b_send.at[0], b_recv.at[0], owner, dev).start()

        def both(step, c):
            for h in range(2):
                step(c, h)

        order = (0, 1, 2, 3, LIFTED, LAST)
        for i, c in enumerate(order):
            if c < PASSED:
                both(first, c)
                if i > 0:
                    both(middle, order[i - 1])
            else:
                if order[i - 1] < PASSED and i > 0:
                    both(middle, order[i - 1])
                both(first, c)
                both(middle, c)
            if i > 1:
                second(order[i - 2])
        second(LIFTED)
        second(LAST)
        arrived(back.at[1], b_recv.at[0])
        finish()
        sent(rows.at[0, 0, 0:2], pay_send.at[0])
        sent(crossed, r_send.at[1])
        sent(done.at[1:CHUNKS], b_send.at[0])

    @pl.when(is_expert)
    def _():
        expert = me // 8

        def is_last(c):
            return isinstance(c, int) and c == LAST

        def widen(c, phase, straight=False):
            landed(c, phase - 1, straight)
            spread(c, phase, straight)

        def share(c, h):
            ref = parts.at[c, h]

            def send(straight):
                for k, step in enumerate((1, 3)):
                    src = band(ref, h, here[h][2], pl.ds(k * QUARTER // 2, QUARTER // 2))
                    dev = line_devs[h][2 if straight else step]
                    remote(src, turned.at[c, h, k], p_send.at[0], p_recv.at[c, h], 2, dev).start()
                    if straight:
                        src = band(ref, h, here[h][step])
                        remote(src, passed.at[c, h, 1 - k], p_send.at[2], r_recv.at[c, h], 2, line_devs[h][step]).start()

            if is_last(c):
                send(True)
            else:
                send(True)
            own = band(ref, h, here[h][0])
            remote(own, own, p_send.at[1], own_recv.at[c, h], 2, me).start()

        for c in range(DIRECT):
            arrived(rows.at[c, y, x], pay_recv.at[c])
            spread(c, 0, False)
        widen(FIRST, 1, True)
        sent(rows.at[FIRST, 0:3], g_send.at[2])
        widen(SECOND, 1, True)
        widen(2, 1)
        pltpu.make_async_copy(wide, wide, w_sems.at[0]).wait()
        pltpu.make_async_copy(wdown, wdown, w_sems.at[1]).wait()
        lane = lax.broadcasted_iota(jnp.int32, (ROW, LANES), 1)
        mine = (lane == expert) | (lane == expert + EXP)

        def unfold(c):
            for i in range(8):
                pair = [rows[c, i // 2, 2 * (i % 2) + k].astype(F32) for k in range(2)]
                to = slice(i * 2 * ROW, (i + 1) * 2 * ROW)
                for k in range(4):
                    row, begin = (k % 2) * ROW, (k // 2) * QUARTER
                    piece = [p[row : row + ROW, begin : begin + QUARTER] for p in pair]
                    block[to, k * QUARTER : (k + 1) * QUARTER] = jnp.concatenate(piece, axis=0).astype(BF16)
                table = [jnp.where(mine, p[0:ROW, HALF:FOLD], 0.0) for p in pair]
                table = [jnp.broadcast_to(jnp.sum(t, axis=1, keepdims=True), (ROW, LANES)) for t in table]
                weight[to, :] = jnp.concatenate(table, axis=0)

        def lift():
            for n in range(TILES):
                both = jnp.dot(block[...], wide[n], preferred_element_type=F32)
                g, u = both[:, 0:LANES], both[:, LANES:]
                hidden[:, n * LANES : (n + 1) * LANES] = (g * u / (1.0 + jnp.exp(-g)) * weight[...]).astype(BF16)

        def lower(c, h):
            made = jnp.dot(hidden[...], wdown[:, h * HALF : (h + 1) * HALF], preferred_element_type=F32)
            made = made.reshape(16, ROW, HALF)
            made = jnp.concatenate([made[:, :, 0:QUARTER], made[:, :, QUARTER:HALF]], axis=1)
            parts[c, h] = made.astype(BF16).reshape(4, 4, 2 * ROW, QUARTER)

        def batch(i, carry):
            c = jnp.where(i < LAST, i, LIFTED)
            after = jnp.where(i < LAST - 1, i + 1, jnp.where(i < LAST, LIFTED, LAST))

            @pl.when(i + 3 < DIRECT)
            def _():
                widen(jnp.minimum(i + 3, DIRECT - 1), 1)

            lift()

            @pl.when(i + 2 < DIRECT)
            def _():
                widen(jnp.minimum(i + 2, DIRECT - 1), 2)

            lower(c, 0)
            share(c, 0)

            @pl.when(i + 1 == SECOND)
            def _():
                landed(SECOND, 1, True)

            @pl.when((i + 1 > SECOND) & (i != LAST - 1))
            def _():
                landed(jnp.minimum(after, LAST), 2, False)

            @pl.when(i == LAST - 1)
            def _():
                arrived(rows.at[LIFTED], g_recv.at[LIFTED, 2])

            unfold(after)
            lower(c, 1)
            share(c, 1)
            return carry

        landed(FIRST, 1, True)
        unfold(FIRST)
        lax.fori_loop(0, CHUNKS - 1, batch, 0)
        lift()
        for h in range(2):
            lower(LAST, h)
            share(LAST, h)
        out[...] = jnp.zeros_like(out)
        sent(rows.at[0:DIRECT, 0, 0:3], g_send.at[0])
        sent(rows.at[2:DIRECT, 0:3], g_send.at[1])
        sent(rows.at[SECOND, 0:3], g_send.at[2])
        sent(turned, p_send.at[0])
        sent(turned, p_send.at[1])
        sent(passed.at[PASSED:CHUNKS], p_send.at[2])


def local(
    query, new_key, new_value, cache_key, cache_value, lengths, residual,
    norm_gain, router_weight, gate_weight, up_weight, down_weight, slot_rows, slot_count,
):
    vmem, smem, hbm = (
        pl.BlockSpec(memory_space=pltpu.VMEM),
        pl.BlockSpec(memory_space=pltpu.SMEM),
        pl.BlockSpec(memory_space=pl.ANY),
    )
    dma = pltpu.SemaphoreType.DMA
    return pl.pallas_call(
        kernel,
        out_shape=jax.ShapeDtypeStruct(query.shape, BF16),
        in_specs=[vmem, vmem, vmem, hbm, hbm, smem, vmem, vmem, vmem, hbm, hbm, hbm, smem, smem],
        out_specs=vmem,
        scratch_shapes=[
            pltpu.VMEM((ROW, CTX, KVH * HD), BF16),
            pltpu.VMEM((ROW, CTX, KVH * HD), BF16),
            pltpu.VMEM((ROW, D), F32),
            pltpu.VMEM((2 * ROW, FOLD), BF16),
            pltpu.VMEM((2, 2, 2 * ROW, QUARTER), BF16),
            pltpu.VMEM((CHUNKS, 2, 2 * ROW, QUARTER), BF16),
            pltpu.VMEM((CHUNKS, 4, 4, 2 * ROW, FOLD), BF16),
            pltpu.VMEM((CHUNKS, 2, 4, 4, 2 * ROW, QUARTER), BF16),
            pltpu.VMEM((CHUNKS, 2, 2, 4, 2 * ROW, QUARTER // 2), BF16),
            pltpu.VMEM((CHUNKS, 2, 2, 4, 2 * ROW, QUARTER), BF16),
            pltpu.VMEM((CHUNKS, 2, 4, 2 * ROW, QUARTER), BF16),
            pltpu.VMEM((CHUNKS, 2, 3, 2 * ROW, QUARTER), BF16),
            pltpu.VMEM((TILES, D, 2 * LANES), BF16),
            pltpu.VMEM((UNITS, D), BF16),
            pltpu.VMEM((BATCH, D), BF16),
            pltpu.VMEM((BATCH, LANES), F32),
            pltpu.VMEM((BATCH, UNITS), BF16),
            dma((2, 2)),
            dma((2,)),
            dma((1,)),
            dma((CHUNKS,)),
            dma((3,)),
            dma((CHUNKS, 3)),
            dma((3,)),
            dma((CHUNKS, 2)),
            dma((CHUNKS, 2)),
            dma((2,)),
            dma((CHUNKS, 3)),
            dma((1,)),
            dma((1,)),
        ],
        compiler_params=pltpu.CompilerParams(
            collective_id=0, has_side_effects=True, vmem_limit_bytes=56 * 2**20
        ),
        name="moe_block",
    )(
        query, new_key, new_value, cache_key, cache_value, lengths, residual,
        norm_gain.reshape(1, D), jnp.transpose(router_weight),
        gate_weight, up_weight, down_weight, slot_rows, slot_count,
    )


def solution(mesh):
    return jax.shard_map(
        local,
        mesh=mesh,
        in_specs=(
            P("side", "dev", None, None),
            P("side", "dev", None, None),
            P("side", "dev", None, None),
            P("side", "dev", None, None, None),
            P("side", "dev", None, None, None),
            P("side", "dev", None),
            P("side", "dev", None, None),
            P(),
            P(),
            P("side", None, "dev"),
            P("side", None, "dev"),
            P("side", "dev", None),
            P("side", "dev", None, None),
            P("side", "dev", None),
        ),
        out_specs=P("side", "dev", None, None),
        check_vma=False,
    )
```
